128 devices in a mesh: seq: 16 (over z, y_hi, core), head: 8 (over x, y_lo).
Axes of the slice: x: 4, y: 4 (y_hi: 2, y_lo: 2; y = y_hi * 2 + y_lo), z: 4, core: 2. Of those that a mesh axis runs over, the one named last changes fastest.
Arguments:
- layer_input: bfloat16 [16384, 1024], P(('seq', 'head')), may hold values from -6 to 6
- shared_weight: bfloat16 [1024, 536], P(('seq', 'head')), may hold values from -0.1875 to 0.1875
- mixer_gain: bfloat16 [1024], P(('seq', 'head')), may hold values from 0.5 to 1.5
- feed_gain: bfloat16 [1024], P(('seq', 'head')), may hold values from 0.5 to 1.5
- branch_weight: bfloat16 [1024, 2, 1536], P('seq', None, 'head'), may hold values from -0.1875 to 0.1875
- query_weight: bfloat16 [1024, 512], P('seq', 'head'), may hold values from -0.375 to 0.375
- mamba_weight: bfloat16 [1024, 1536], P('seq', 'head'), may hold values from -0.15625 to 0.15625
- attend_weight: bfloat16 [1024, 512], P('seq', 'head'), may hold values from -3 to 3
- hidden_weight: bfloat16 [1024, 2, 2048], P('seq', None, 'head'), may hold values from -0.1875 to 0.1875
- down_weight: bfloat16 [1024, 2048], P('seq', 'head'), may hold values from -0.125 to 0.125
- rate_log: float32 [24], P('head'), may hold values from -10 to 0
- step_bias: float32 [24], P('head'), may hold values from -6 to 0
- mamba_gain: float32 [1536], P('head'), may hold values from 0.5 to 1.5
- cotangent: bfloat16 [16384, 1024], P(('seq', 'head')), may hold values from -6 to 6
Outputs:
- layer_output: bfloat16 [16384, 1024], P(('seq', 'head'))
- input_grad: float32 [16384, 1024], P(('seq', 'head'))
- shared_grad: float32 [1024, 536], P(('seq', 'head'))
- mixer_gain_grad: float32 [1024], P(('seq', 'head'))
- feed_gain_grad: float32 [1024], P(('seq', 'head'))
- branch_grad: float32 [1024, 2, 1536], P('seq', None, 'head')
- query_grad: float32 [1024, 512], P('seq', 'head')
- mamba_grad: float32 [1024, 1536], P('seq', 'head')
- attend_grad: float32 [1024, 512], P('seq', 'head')
- hidden_grad: float32 [1024, 2, 2048], P('seq', None, 'head')
- down_grad: float32 [1024, 2048], P('seq', 'head')
- rate_log_grad: float32 [24], P('head')
- step_bias_grad: float32 [24], P('head')
- mamba_gain_grad: float32 [1536], P('head')
The draws below stay inside these ranges and needn't reach their ends.
All inputs are finite; a program needn't handle non-finite values.
Results may differ from the reference program's by a relative error of at most 0.04.
Values may be sent and summed in bfloat16 or wider, within the bound.
No kernel may reach another device: no remote copies, remote signals or barrier semaphores. Data moves between devices by JAX's collectives and lax.ppermute only.
A program may use at most 192 MiB of HBM per device.

```python
import math
import jax
import jax.numpy as jnp
from jax import lax

D = 1024
FF = 2048
SSM_HEADS = 24
SSM_DIM = 64
STATE = 128
ATT_HEADS = 8
KV_HEADS = 2
HEAD_DIM = 64
SHARED = 536
TOKENS = 16384


def levels(stream_key, dims, cuts, low, high):
    def one(dim, shards_of):
        draws = jax.random.uniform(jax.random.fold_in(jax.random.fold_in(stream_key, 6), dim), (shards_of,), jnp.float32, low / len(cuts), high / len(cuts))
        return jnp.repeat(jnp.exp(draws), dims[dim] // shards_of).reshape((-1,) + (1,) * (len(dims) - dim - 1))

    loudness = one(*cuts[0])
    for cut in cuts[1:]:
        loudness = loudness * one(*cut)
    return loudness


def gaussian(rng, dims, deviation, limit, pieces=(), kind=jnp.bfloat16):
    loudness = levels(rng, dims, pieces, -0.22, 0.18) if pieces else 1.0
    values = jax.random.normal(rng, dims, jnp.float32) * deviation * loudness
    return jnp.minimum(jnp.maximum(values, -limit), limit).astype(kind)


def setup_inputs(seed: int = 0) -> dict:
    seeds = jax.random.split(jax.random.key(seed), 15)
    layer_input = gaussian(seeds[0], (TOKENS, D), 1.0, 6.0, ((0, 128),))
    shared_weight = gaussian(seeds[1], (D, SHARED), D ** -0.5, 0.1875, ((0, 128),))
    mixer_gain = jnp.clip(1.0 + 0.1 * jax.random.normal(seeds[2], (D,), jnp.float32), 0.5, 1.5).astype(jnp.bfloat16)
    feed_gain = jnp.clip(1.0 + 0.1 * jax.random.normal(seeds[3], (D,), jnp.float32), 0.5, 1.5).astype(jnp.bfloat16)
    branch_weight = gaussian(seeds[4], (D, 2, SSM_HEADS * SSM_DIM), D ** -0.5, 0.1875, ((0, 16), (2, 8)))
    query_weight = gaussian(seeds[5], (D, ATT_HEADS * HEAD_DIM), (D // 4) ** -0.5, 0.375, ((0, 16), (1, 8)))
    mamba_weight = gaussian(seeds[6], (D, SSM_HEADS * SSM_DIM), (SSM_HEADS * SSM_DIM) ** -0.5, 0.15625, ((0, 16), (1, 8)))
    attend_weight = gaussian(seeds[7], (D, ATT_HEADS * HEAD_DIM), (HEAD_DIM // 16) ** -0.5, 3.0, ((0, 16), (1, 8)))
    hidden_weight = gaussian(seeds[8], (D, 2, FF), D ** -0.5, 0.1875, ((0, 16), (2, 8)))
    down_weight = gaussian(seeds[9], (D, FF), FF ** -0.5, 0.125, ((0, 16), (1, 8)))
    rate_log = jnp.clip(-10.0 + 10.0 * jax.random.uniform(seeds[10], (SSM_HEADS,), jnp.float32) ** levels(seeds[10], (SSM_HEADS,), ((0, 8),), -0.2, 0.2), -10.0, 0.0)
    step_bias = jnp.clip(-6.0 + 6.0 * jax.random.uniform(seeds[11], (SSM_HEADS,), jnp.float32) ** levels(seeds[11], (SSM_HEADS,), ((0, 8),), -0.2, 0.2), -6.0, 0.0)
    mamba_gain = jnp.clip(1.0 + 0.1 * jax.random.normal(seeds[12], (SSM_HEADS * SSM_DIM,), jnp.float32), 0.5, 1.5)
    cotangent = gaussian(seeds[13], (TOKENS, D), 1.0, 6.0, ((0, 128),))
    return dict(layer_input=layer_input, shared_weight=shared_weight, mixer_gain=mixer_gain, feed_gain=feed_gain, branch_weight=branch_weight, query_weight=query_weight, mamba_weight=mamba_weight, attend_weight=attend_weight, hidden_weight=hidden_weight, down_weight=down_weight, rate_log=rate_log, step_bias=step_bias, mamba_gain=mamba_gain, cotangent=cotangent)


@jax.custom_vjp
def low(v):
    return lax.optimization_barrier(v.astype(jnp.bfloat16)).astype(jnp.float32)

@jax.custom_vjp
def low_back(v):
    return v

def low_keep(v):
    return (low(v), None)

def low_pass(kept, grad):
    return (grad,)

def back_keep(v):
    return (v, None)

def back_low(kept, grad):
    return (low(grad),)
low.defvjp(low_keep, low_pass)
low_back.defvjp(back_keep, back_low)
norm_eps = 1e-05
highest = lax.Precision.HIGHEST
masked_score = -1e+30

def rms_rows(values, gain):
    return values * lax.rsqrt(lax.optimization_barrier(jnp.mean(values * values, axis=-1, keepdims=True)) + norm_eps) * gain

def swish(values):
    return values * lax.logistic(values)

def softplus_smooth(values):
    return jnp.log1p(jnp.exp(-jnp.abs(values))) + jnp.maximum(values, 0.0)

def scan_block(carry_state, block_data):
    inputs, write_rows, read_rows, step_sizes, log_decay = block_data
    cumulative = jnp.cumsum(log_decay, axis=0)
    spread = cumulative[:, None, :] - cumulative[None, :, :]
    causal = lax.broadcasted_iota(jnp.int32, spread.shape, 0) >= lax.broadcasted_iota(jnp.int32, spread.shape, 1)
    decays = jnp.where(causal, jnp.exp(jnp.where(causal, spread, 0.0)), 0.0)
    products = jnp.dot(read_rows, write_rows.T, precision=highest)
    weights = decays * products[:, :, None] * step_sizes[None, :, :]
    within = jnp.einsum('tsh,shp->thp', weights, inputs, precision=highest)
    carried = jnp.exp(cumulative)[:, :, None] * jnp.einsum('tn,hpn->thp', read_rows, carry_state, precision=highest)
    tail_weights = jnp.exp(cumulative[-1][None, :] - cumulative) * step_sizes
    fresh_state = jnp.einsum('sh,shp,sn->hpn', tail_weights, inputs, write_rows, precision=highest)
    return (jnp.exp(cumulative[-1])[:, None, None] * carry_state + fresh_state, within + carried)

def ssm_scan(inputs, write_rows, read_rows, step_sizes, log_decay, block_size):
    block_count = inputs.shape[0] // block_size
    blocks = tuple((member.reshape((block_count, block_size) + member.shape[1:]) for member in (inputs, write_rows, read_rows, step_sizes, log_decay)))
    start_state = jnp.zeros((inputs.shape[1], inputs.shape[2], write_rows.shape[1]), jnp.float32)
    final_state, outputs = lax.scan(jax.checkpoint(scan_block), start_state, blocks)
    return outputs.reshape(inputs.shape)

def attention(queries, keys, values):
    total_rows = queries.shape[0]
    group_size = ATT_HEADS // KV_HEADS
    keys_wide = jnp.repeat(keys, group_size, axis=1)
    values_wide = jnp.repeat(values, group_size, axis=1)
    block_rows = math.gcd(total_rows, 512)
    positions = lax.broadcasted_iota(jnp.int32, (total_rows,), 0)

    def attend_block(packed):
        query_block, first_row = packed
        scores = low_back(jnp.einsum('qhd,khd->hqk', query_block, keys_wide, precision=highest) * HEAD_DIM ** (-0.5))
        rows_at = first_row + lax.broadcasted_iota(jnp.int32, (block_rows,), 0)
        visible = positions[None, :] <= rows_at[:, None]
        scores = jnp.where(visible[None], scores, masked_score)
        row_peak = lax.optimization_barrier(jnp.max(scores, axis=-1, keepdims=True))
        exponent = jnp.exp(scores - row_peak)
        probabilities = low(exponent / lax.optimization_barrier(jnp.sum(exponent, axis=-1, keepdims=True)))
        return jnp.einsum('hqk,khd->qhd', probabilities, values_wide, precision=highest)
    query_blocks = queries.reshape(total_rows // block_rows, block_rows, ATT_HEADS, HEAD_DIM)
    firsts = jnp.arange(total_rows // block_rows, dtype=jnp.int32) * block_rows
    outputs = lax.map(jax.checkpoint(attend_block), (query_blocks, firsts))
    return outputs.reshape(total_rows, ATT_HEADS, HEAD_DIM)

def forward_layer(layer_input, shared_weight, mixer_gain, feed_gain, branch_weight, query_weight, mamba_weight, attend_weight, hidden_weight, down_weight, rate_log, step_bias, mamba_gain):
    total_rows = layer_input.shape[0]
    kv_width = KV_HEADS * HEAD_DIM
    normed = low(rms_rows(layer_input, mixer_gain))
    shared = low(low_back(jnp.dot(normed, shared_weight, precision=highest)))
    write_rows = shared[:, :STATE]
    read_rows = shared[:, STATE:2 * STATE]
    keys = shared[:, 2 * STATE:2 * STATE + kv_width].reshape(total_rows, KV_HEADS, HEAD_DIM)
    values = shared[:, 2 * STATE + kv_width:2 * STATE + 2 * kv_width].reshape(total_rows, KV_HEADS, HEAD_DIM)
    step_raw = shared[:, 2 * STATE + 2 * kv_width:]
    branch = low_back(jnp.dot(normed, branch_weight.reshape(D, 2 * SSM_HEADS * SSM_DIM), precision=highest))
    branch = branch.reshape(total_rows, 2, SSM_HEADS, SSM_DIM)
    inputs = low(branch[:, 0])
    gate_in = branch[:, 1]
    queries = low(low_back(jnp.dot(normed, query_weight, precision=highest))).reshape(total_rows, ATT_HEADS, HEAD_DIM)
    step_sizes = softplus_smooth(step_raw + step_bias)
    log_decay = -jnp.exp(rate_log) * step_sizes
    mamba_y = ssm_scan(inputs, write_rows, read_rows, step_sizes, log_decay, math.gcd(total_rows, 256))
    gated_out = mamba_y * swish(gate_in)
    mamba_norm = gated_out * lax.rsqrt(lax.optimization_barrier(jnp.mean(gated_out * gated_out, axis=-1, keepdims=True)) + norm_eps) * mamba_gain.reshape(SSM_HEADS, SSM_DIM)
    mamba_low = low(mamba_norm.reshape(total_rows, SSM_HEADS * SSM_DIM))
    attend_low = low(low_back(attention(queries, keys, values))).reshape(total_rows, ATT_HEADS * HEAD_DIM)
    mixed_out = low_back(jnp.dot(mamba_low, mamba_weight.T, precision=highest) + jnp.dot(attend_low, attend_weight.T, precision=highest))
    residual = layer_input + mixed_out
    feed_in = low(rms_rows(residual, feed_gain))
    hidden = low_back(jnp.dot(feed_in, hidden_weight.reshape(D, 2 * FF), precision=highest)).reshape(total_rows, 2, FF)
    hidden_units = low(swish(hidden[:, 0]) * hidden[:, 1])
    return residual + low_back(jnp.dot(hidden_units, down_weight.T, precision=highest))

def reference(layer_input, shared_weight, mixer_gain, feed_gain, branch_weight, query_weight, mamba_weight, attend_weight, hidden_weight, down_weight, rate_log, step_bias, mamba_gain, cotangent):
    params = tuple((member.astype(jnp.float32) for member in (layer_input, shared_weight, mixer_gain, feed_gain, branch_weight, query_weight, mamba_weight, attend_weight, hidden_weight, down_weight, rate_log, step_bias, mamba_gain)))
    result, pullback = jax.vjp(forward_layer, *params)
    grads = pullback(cotangent.astype(jnp.float32))
    return (result.astype(jnp.bfloat16), grads[0], grads[1], grads[2], grads[3], grads[4], grads[5], grads[6], grads[7], grads[8], grads[9], grads[10], grads[11], grads[12])
```

```python
import jax
import jax.numpy as jnp
from jax import lax
from jax.experimental import pallas as pl
from jax.experimental.pallas import tpu as pltpu
from jax.sharding import PartitionSpec as P

HEAD_DIM = 64
STATE = 128
ATT_HEADS = 8
KV_HEADS = 2
HEADS = 3
SPAN = 1024
GRAD_ROWS = 256
FEED_ROWS = 512
KEYS = 512
BACK_KEYS = 256
PER = 2
ROWS = 512
CHUNK = 256
SPANS = 16
CHIPS = 8
SEQ = ("chip", "core")
WIDE = 256
PACK = 1280

norm_eps = 1e-05
masked_score = -1e30
f32, bf16 = jnp.float32, jnp.bfloat16
MIB = 1024 * 1024


def gather(part, axis):
    size = lax.axis_size(axis)
    return lax.all_to_all(jnp.broadcast_to(part[None], (size,) + part.shape), axis, 0, 0)


def beside_y(part):
    return lax.ppermute(part, "head", [(k, k ^ 1) for k in range(8)])


def along_x(pairs):
    return [pairs[0]] + [
        lax.ppermute(pairs[d], "head", [(k, (k + 2 * d) % 8) for k in range(8)])
        for d in (1, 2, 3)
    ]


def shift_x(part, distance):
    return lax.ppermute(part, "head", [(k, (k + 2 * distance) % 8) for k in range(8)])


def near_x(own, beside):
    return [shift_x(own, 1), shift_x(beside, 1), shift_x(own, 3), shift_x(beside, 3)]


def relayed(own, beside, near):
    far = [shift_x(near[0], 1), shift_x(near[3], 3)]
    return [own, beside, *near[:2], *far, *near[2:]]


def other_core(part):
    return lax.ppermute(part, "core", [(0, 1), (1, 0)])


def exchange(pieces, axis):
    return lax.all_to_all(pieces, axis, 0, 0)


def rows(stacked):
    return stacked.reshape((-1,) + stacked.shape[2:])


def whole(*shape):
    return pl.BlockSpec(shape, lambda i, ids: (0,) * len(shape))


def blocks(*shape):
    return pl.BlockSpec(shape, lambda i, ids: (i,) + (0,) * (len(shape) - 1))


def lanes(*shape):
    return pl.BlockSpec(shape, lambda i, ids: (0,) * (len(shape) - 1) + (i,))


def backwards(spec, steps):
    index = spec.index_map
    return pl.BlockSpec(spec.block_shape, lambda i, ids: index(steps - 1 - i, ids))


def kernel_call(body, grid, ids, ins, outs, scratch=(), flops=0, limit=60):
    arrays, in_specs = zip(*ins)
    shapes, out_specs = zip(*outs)
    moved = sum(a.size * a.dtype.itemsize for a in arrays) + sum(
        s.size * s.dtype.itemsize for s in shapes
    )
    return pl.pallas_call(
        body,
        grid_spec=pltpu.PrefetchScalarGridSpec(
            num_scalar_prefetch=1,
            grid=(grid,),
            in_specs=list(in_specs),
            out_specs=list(out_specs),
            scratch_shapes=list(scratch),
        ),
        out_shape=list(shapes),
        compiler_params=pltpu.CompilerParams(
            dimension_semantics=("arbitrary",), vmem_limit_bytes=limit * MIB
        ),
        cost_estimate=pl.CostEstimate(flops=flops, bytes_accessed=moved, transcendentals=0),
    )(ids, *arrays)


def shape(*dims, kind=f32):
    return jax.ShapeDtypeStruct(dims, kind)


def dot(a, b):
    return jnp.dot(a, b, preferred_element_type=f32)


def dot_nt(a, b):
    return lax.dot_general(a, b, (((1,), (1,)), ((), ())), preferred_element_type=f32)


def dot_tn(a, b):
    return lax.dot_general(a, b, (((0,), (0,)), ((), ())), preferred_element_type=f32)


def select_sum(a, b):
    high = a.astype(bf16)
    return dot(high, b) + dot((a - high.astype(f32)).astype(bf16), b)


def iota(dims, axis):
    return lax.broadcasted_iota(jnp.int32, dims, axis)


def spread(columns, base):
    lane = iota((columns.shape[0], WIDE), 1)
    c = [columns[:, base + h : base + h + 1] for h in range(HEADS)]
    return jnp.where(
        lane < 64, c[0], jnp.where(lane < 128, c[1], jnp.where(lane < 192, c[2], 0.0))
    )


def spread_rows(parts):
    row = iota((WIDE, STATE), 0)
    return jnp.where(
        row < 64, parts[0], jnp.where(row < 128, parts[1], jnp.where(row < 192, parts[2], 0.0))
    )


def head_select(offset):
    lane, column = iota((WIDE, 128), 0), iota((WIDE, 128), 1)
    return jnp.where((column == offset + lane // 64) & (lane < 192), 1.0, 0.0).astype(bf16)


def head_mean(values):
    a, b = iota((WIDE, WIDE), 0), iota((WIDE, WIDE), 1)
    return select_sum(values, jnp.where(a // 64 == b // 64, 1.0 / 64, 0.0).astype(bf16))


def prefix_sum(values):
    width = values.shape[1]
    lane = iota(values.shape, 1)
    step = 1
    while step < width:
        values = values + jnp.where(lane >= step, pltpu.roll(values, step, 1), 0.0)
        step *= 2
    return values


def suffix_sum(values):
    width = values.shape[1]
    lane = iota(values.shape, 1)
    step = 1
    while step < width:
        values = values + jnp.where(lane < width - step, pltpu.roll(values, width - step, 1), 0.0)
        step *= 2
    return values


def columns_of(parts):
    n = parts[0].shape[1]
    full = jnp.concatenate(list(parts) + [jnp.zeros((128 - 8 * len(parts), n), f32)], axis=0)
    return full.T


def by_distance(refs):
    if len(refs) == 8:
        return list(zip(refs[0::2], refs[1::2]))
    return [(ref.at[0], ref.at[1]) for ref in refs]


def span_rows(ids, first, refs, tokens):
    head = ids[1]
    beside = lax.rem(head, 2)
    for n in range(tokens.shape[0] // 256):
        distance = lax.rem(head // 2 - (first + n) + 4, 4)
        mine = pl.multiple_of(256 * n + 128 * beside, 128)
        theirs = pl.multiple_of(256 * n + 128 - 128 * beside, 128)
        for d, pair in enumerate(by_distance(refs)):

            @pl.when(distance == d)
            def _(pair=pair, mine=mine, theirs=theirs):
                tokens[pl.ds(mine, 128), :] = pair[0][...]
                tokens[pl.ds(theirs, 128), :] = pair[1][...]


def project_kernel(ids, *refs):
    inputs, (same, other, params) = refs[:8], refs[8:11]
    normed, x_out, gate_out, wr_out, q_out, col_out, row_out = refs[11:18]
    states, pack, gains, weights, carry, total, tokens = refs[18:]
    i = pl.program_id(0)
    head = ids[1]
    kv_head = head // (ATT_HEADS // KV_HEADS)

    @pl.when(i == 0)
    def _():
        carry[...] = jnp.zeros_like(carry)
        total[...] = jnp.zeros_like(total)
        for c in range(CHIPS):
            for part, core in ((same, ids[3]), (other, 1 - ids[3])):
                first = pl.multiple_of((2 * c + core) * 64, 64)
                weights[pl.ds(first, 64), :] = part[c, :, :1024]
        gains[...] = weights[:, 384:512].astype(f32).T[88:96]
        for c in range(CHIPS):
            pack[c, SPAN:, :] = jnp.zeros((PACK - SPAN, 128), bf16)

    span_rows(ids, PER * i, inputs, tokens)
    values = tokens[...].astype(f32)
    scale = lax.rsqrt(jnp.mean(values * values, axis=1, keepdims=True) + norm_eps)
    low = (values * scale * gains[0:1, :]).astype(bf16)
    normed[...] = low
    made = dot(low, weights[...])
    wide_lane = iota((ROWS, WIDE), 1)
    lane = iota((ROWS, 128), 1)
    x = jnp.where(wide_lane < 192, made[:, :256], 0.0).astype(bf16)
    x_out[...] = x
    gate_out[...] = jnp.where(wide_lane < 192, made[:, 256:512], 0.0)
    q = pltpu.roll(made[:, 128:256], 64, 1)
    q_out[...] = jnp.where(lane < 64, q.astype(bf16).astype(f32) * HEAD_DIM**-0.5, 0.0).astype(bf16)
    write = made[:, 512:640].astype(bf16)
    wr_out[:, :128] = write
    wr_out[:, 128:] = made[:, 640:768].astype(bf16)
    keys, vals = made[:, 768:896], made[:, 896:1024]
    first = kv_head == 0
    keys = jnp.where(first, keys, pltpu.roll(keys, 64, 1))
    vals = jnp.where(first, pltpu.roll(vals, 64, 1), vals)
    kv = jnp.where(lane < 64, keys, vals).astype(bf16)
    for c in range(CHIPS):
        pack[c, pl.ds(pl.multiple_of(i * ROWS, ROWS), ROWS), :] = kv

    misc = made[:, 384:512].astype(bf16).astype(f32)
    raws = pltpu.roll(misc, 64 - HEADS * head, 1).T[:8]
    own = iota((8, ROWS), 0) < HEADS
    z = jnp.where(own, raws, 0.0) + params[:, 0:1]
    step = jnp.where(own, jnp.log1p(jnp.exp(-jnp.abs(z))) + jnp.maximum(z, 0.0), 0.0)
    log_decay = -jnp.exp(params[:, 1:2]) * step
    row_out[8:16, :] = step
    row_out[16:24, :] = lax.logistic(z)
    parts = []
    for c in range(PER):
        here = slice(c * CHUNK, c * CHUNK + CHUNK)
        cum = prefix_sum(log_decay[:, here])
        row_out[0:8, here] = cum
        columns = columns_of([cum, step[:, here]])
        col_out[here, :] = columns
        last = cum[:, CHUNK - 1 : CHUNK]
        tail = jnp.exp(spread_last(last) - spread(columns, 0)) * spread(columns, 8)
        fresh = dot_tn((x[here].astype(f32) * tail).astype(bf16), write[here])
        parts.append((last, fresh))
    state, passed = carry[...], total[...]
    for c, (last, fresh) in enumerate(parts):
        states[c] = state
        grown = jnp.exp(last)
        state = spread_rows([grown[h : h + 1] for h in range(HEADS)]) * state + fresh
        passed = passed + jnp.broadcast_to(last, (8, 128))
    carry[...] = state
    total[...] = passed

    @pl.when(i == pl.num_programs(0) - 1)
    def _():
        state = carry[:192].astype(bf16)
        high = total[...].astype(bf16).astype(f32)
        decays = jnp.concatenate([high, total[...] - high], axis=0).astype(bf16)
        for c in range(CHIPS):
            pack[c, SPAN : SPAN + 192, :] = state
            pack[c, SPAN + 192 : SPAN + 208, :] = decays


def spread_last(last):
    lane = iota((1, WIDE), 1)
    return jnp.where(
        lane < 64,
        last[0:1],
        jnp.where(lane < 128, last[1:2], jnp.where(lane < 192, last[2:3], 0.0)),
    )


def combine_states(span_of, place, later):
    passed = jnp.zeros((8, 128), f32)
    entry = jnp.zeros((192, 128), f32)
    row = iota((192, 128), 0)
    order = range(SPANS) if later else reversed(range(SPANS))
    for k in order:
        use = (k > place) if later else (k < place)
        weight = jnp.where(use, jnp.exp(passed), 0.0)
        weights = jnp.where(
            row < 64, weight[0:1], jnp.where(row < 128, weight[1:2], weight[2:3])
        )
        span = span_of(k).astype(f32)
        entry = entry + weights * span[0:192]
        decay = span[192:200] + span[200:208]
        passed = passed + jnp.where(use, decay, 0.0)
    return jnp.concatenate([entry, jnp.zeros((64, 128), f32)], axis=0)


def scan_kernel(
    ids, x_ref, gate_ref, wr_ref, col_ref, row_ref, local, same, other, gain,
    y_out, low_out, state_out,
    carried,
):
    i = pl.program_id(0)

    @pl.when(i == 0)
    def _():
        carried[...] = combine_states(
            lambda k: jnp.where(ids[3] == k % 2, same[k // 2, :208], other[k // 2, :208]),
            ids[0],
            False,
        )

    passed = carried[...]
    entries = []
    for c in range(PER):
        entries.append(local[c] + passed)
        grown = jnp.exp(row_ref[0:8, c * CHUNK + CHUNK - 1 : c * CHUNK + CHUNK])
        passed = spread_rows([grown[h : h + 1] for h in range(HEADS)]) * passed
    carried[...] = passed
    causal = iota((CHUNK, CHUNK), 0) >= iota((CHUNK, CHUNK), 1)
    wide_lane = iota((CHUNK, WIDE), 1)
    for c, entry in enumerate(entries):
        here = slice(c * CHUNK, c * CHUNK + CHUNK)
        state_out[c] = entry
        columns = col_ref[here, :]
        write, read = wr_ref[here, :128], wr_ref[here, 128:]
        cum = spread(columns, 0)
        scaled = (x_ref[here, :].astype(f32) * spread(columns, 8)).astype(bf16)
        products = dot_nt(read, write)
        y = jnp.exp(cum) * dot_nt(read, entry.astype(bf16))
        for h in range(HEADS):
            span = columns[:, h : h + 1] - row_ref[h : h + 1, here]
            weights = jnp.exp(jnp.where(causal, span, masked_score)) * products
            part = jnp.where(wide_lane // 64 == h, scaled, jnp.zeros_like(scaled))
            y = y + dot(weights.astype(bf16), part)
        y_out[here, :] = y
        gate = gate_ref[here, :]
        gated = y * (gate * lax.logistic(gate))
        low = gated * lax.rsqrt(head_mean(gated * gated) + norm_eps) * gain[...]
        low_out[here, :] = low.astype(bf16)


def attend_visit(kv_ref, q_ref, peak, accum, masked):
    before = now = peak[0:1, :]
    blocks_of = []
    for first in range(0, SPAN, KEYS):
        kv = kv_ref[0, first : first + KEYS, :]
        scores = dot_nt(kv, q_ref[...])
        if masked:
            dims = (KEYS, SPAN)
            scores = jnp.where(iota(dims, 0) + first > iota(dims, 1), masked_score, scores)
        now = jnp.maximum(now, jnp.max(scores, axis=0, keepdims=True))
        blocks_of.append((kv, scores))
    total = accum[...] * jnp.exp(before - now)
    for kv, scores in blocks_of:
        ones = jnp.where(iota(kv.shape, 1) < 64, jnp.ones_like(kv), kv)
        total = total + dot_tn(ones, jnp.exp(scores - now).astype(bf16))
    accum[...] = total
    peak[...] = jnp.broadcast_to(now, peak.shape)


def attend_same_kernel(ids, q_ref, kv_ref, peak, accum):
    k = pl.program_id(0)

    @pl.when(k == 0)
    def _():
        peak[...] = jnp.full_like(peak, masked_score)
        accum[...] = jnp.zeros_like(accum)

    @pl.when(k < ids[2])
    def _():
        attend_visit(kv_ref, q_ref, peak, accum, False)

    @pl.when(k == ids[2])
    def _():
        attend_visit(kv_ref, q_ref, peak, accum, True)


def attend_other_kernel(
    ids, q_ref, kv_ref, low_ref, peak_in, accum_in, mix_out, o_out, lse_out, peak, accum
):
    k = pl.program_id(0)

    @pl.when(k == 0)
    def _():
        peak[...] = peak_in[...]
        accum[...] = accum_in[...]

    @pl.when(k < ids[2] + ids[3])
    def _():
        attend_visit(kv_ref, q_ref, peak, accum, False)

    @pl.when(k == pl.num_programs(0) - 1)
    def _():
        lane = iota((SPAN, 128), 1)
        total = accum[0:1, :]
        out = (accum[...] / total).T
        o_out[...] = out
        mix_out[:, :128] = low_ref[:, :128]
        mix_out[:, 128:] = jnp.where(lane < 64, low_ref[:, 128:], out.astype(bf16))
        lse_out[...] = peak[...] + jnp.log(total)


def by_head(ids, refs):
    head = ids[1]
    for d, pair in enumerate(by_distance(refs)):
        x = lax.rem(head // 2 - d + 4, 4)
        for t in range(2):
            yield 2 * x + lax.rem(head + t, 2), pair[t]


def residual_kernel(ids, mix, *refs):
    weight_refs, (inp, gains, residual_out, feed_out) = refs[:8], refs[8:]
    total = jnp.zeros(residual_out.shape, f32)
    for h, weights in by_head(ids, weight_refs):
        total = total + dot_nt(mix[h], weights[...])
    residual = inp[...].astype(f32) + total
    residual_out[...] = residual
    scale = lax.rsqrt(jnp.mean(residual * residual, axis=1, keepdims=True) + norm_eps)
    feed = (residual * scale * gains[1:2, :]).astype(bf16)
    for h in range(8):
        feed_out[h] = feed


def by_x(ids, first, part, outs):
    beside = lax.rem(ids[1], 2)
    for n in range(part.shape[0] // 256):
        distance = lax.rem(first + n - ids[1] // 2 + 4, 4)
        for d, out in enumerate(outs):

            @pl.when(distance == d)
            def _(out=out, n=n):
                out[beside] = part[256 * n : 256 * n + 128]
                out[1 - beside] = part[256 * n + 128 : 256 * n + 256]


def feed_kernel(ids, feed, *refs):
    weights, *parts, back_out, units_out, hidden_out, cot = refs[8:]
    first = pl.program_id(0) * (FEED_ROWS // 256)
    span_rows(ids, first, refs[:8], cot)
    hidden = dot(feed[...], weights[:, :512])
    gate, up = hidden[:, :256], hidden[:, 256:]
    sig = lax.logistic(gate)
    swish = gate * sig
    units = (swish * up).astype(bf16)
    units_out[...] = units
    down = weights[:, 512:768]
    part = dot_nt(units, down).astype(bf16)
    by_x(ids, first, part, parts)
    grad_units = dot(cot[...], down)
    grad_gate = grad_units * up * (sig * (1.0 + gate * (1.0 - sig)))
    grad_hidden = jnp.concatenate([grad_gate, grad_units * swish], axis=1).astype(bf16)
    hidden_out[...] = grad_hidden
    back_out[...] = dot_nt(grad_hidden, weights[:, :512]).astype(bf16)


def mixed_kernel(ids, back, residual_ref, cot, gains, *refs):
    weight_refs, (grad_out, copies, gain_out, parts) = refs[:8], refs[8:]
    grad_feed = back[0].astype(f32)
    for h in range(1, 8):
        grad_feed = grad_feed + back[h].astype(f32)
    residual = residual_ref[...]
    scale = lax.rsqrt(jnp.mean(residual * residual, axis=1, keepdims=True) + norm_eps)
    normal = residual * scale
    gain_out[...] = jnp.broadcast_to(
        jnp.sum(grad_feed * normal, axis=0, keepdims=True), gain_out.shape
    )
    w = grad_feed * gains[1:2, :]
    grad = cot[...].astype(f32) + scale * (
        w - normal * jnp.mean(w * normal, axis=1, keepdims=True)
    )
    grad_out[...] = grad
    low = grad.astype(bf16)
    copies[...] = low
    for h, weights in by_head(ids, weight_refs):
        parts[h] = dot(low, weights[...]).astype(bf16)


def gate_back_kernel(
    ids, grad_ref, y_ref, gate_ref, gain, wr_ref, col_ref, row_ref, o_ref, decays,
    gy_out, ggate_out, do_out, delta_out, pack, gain_out,
    carry,
):
    i = pl.program_id(0)

    @pl.when(i == 0)
    def _():
        carry[...] = jnp.zeros_like(carry)
        gain_out[...] = jnp.zeros_like(gain_out)

    wide_lane = iota((ROWS, WIDE), 1)
    lane = iota((ROWS, 128), 1)
    own = wide_lane < 192
    grad_all = grad_ref[...].astype(f32)
    grad = jnp.where(own, grad_all, 0.0)
    grad_out = jnp.where(lane < 64, 0.0, grad_all[:, 128:])
    do_out[...] = grad_out.astype(bf16)
    delta = jnp.sum((grad_out * o_ref[...]).T, axis=0, keepdims=True)
    delta_out[...] = jnp.broadcast_to(delta, (8, ROWS))
    y, gate = y_ref[...], gate_ref[...]
    sig = lax.logistic(gate)
    swish = gate * sig
    m = y * swish
    q = lax.rsqrt(head_mean(m * m) + norm_eps)
    gain_out[...] += jnp.broadcast_to(jnp.sum(grad * m * q, axis=0, keepdims=True), (8, WIDE))
    w = grad * gain[...]
    grad_gated = q * (w - m * (q * q) * head_mean(w * m))
    gy = grad_gated * swish
    gy_out[...] = gy
    ggate_out[...] = (grad_gated * y * (sig * (1.0 + gate * (1.0 - sig)))).astype(bf16)
    weighted = (gy * jnp.exp(spread(col_ref[...], 0))).astype(bf16)
    state = carry[...]
    for c in reversed(range(PER)):
        here = slice(c * CHUNK, c * CHUNK + CHUNK)
        grown = jnp.exp(row_ref[0:8, c * CHUNK + CHUNK - 1 : c * CHUNK + CHUNK])
        state = spread_rows([grown[h : h + 1] for h in range(HEADS)]) * state + dot_tn(
            weighted[here], wr_ref[here, 128:]
        )
    carry[...] = state

    @pl.when(i == pl.num_programs(0) - 1)
    def _():
        state = carry[:192].astype(bf16)
        for c in range(SPANS):
            pack[c, :192, :] = state
            pack[c, 192:208, :] = decays[0, 192:208, :]


def attend_back_visit(refs, masked, arrived=None):
    q_ref, kv_ref, do_ref, lse, delta, dkv_out, accum = refs
    for first in range(0, SPAN, BACK_KEYS):
        here = slice(first, first + BACK_KEYS)
        kv = kv_ref[0, here, :]
        scores = dot_nt(kv, q_ref[...])
        if masked:
            dims = (BACK_KEYS, SPAN)
            scores = jnp.where(iota(dims, 0) + first > iota(dims, 1), masked_score, scores)
        probs = jnp.exp(scores - lse[0:1, :])
        grad_probs = dot_nt(kv, do_ref[...])
        grad_scores = (probs * (grad_probs - delta[0:1, :])).astype(bf16)
        dkv = dot(probs.astype(bf16), do_ref[...]) + dot(grad_scores, q_ref[...])
        if arrived is not None:
            dkv = dkv + arrived[0, here, :].astype(f32)
        dkv_out[0, here, :] = dkv.astype(bf16)
        accum[...] += dot_tn(kv, grad_scores)


def attend_back_other_kernel(ids, q_ref, kv_ref, do_ref, lse, delta, dkv_out, dq_out):
    k = pl.program_id(0)
    seen = ids[2] + ids[3]

    @pl.when(k == 0)
    def _():
        dq_out[...] = jnp.zeros_like(dq_out)

    @pl.when(k < seen)
    def _():
        attend_back_visit((q_ref, kv_ref, do_ref, lse, delta, dkv_out, dq_out), False)

    @pl.when(k >= seen)
    def _():
        dkv_out[...] = jnp.zeros_like(dkv_out)


def attend_back_same_kernel(
    ids, q_ref, kv_ref, do_ref, lse, delta, dq_in, arrived, dkv_out, dq_out, accum
):
    k = pl.program_id(0)
    refs = (q_ref, kv_ref, do_ref, lse, delta, dkv_out, accum)

    @pl.when(k == 0)
    def _():
        accum[...] = dq_in[...]

    @pl.when(k < ids[2])
    def _():
        attend_back_visit(refs, False, arrived)

    @pl.when(k == ids[2])
    def _():
        attend_back_visit(refs, True, arrived)
        dq = pltpu.roll((accum[...] * HEAD_DIM**-0.5).T, 64, 1)
        dq_out[...] = jnp.where(iota((SPAN, 128), 1) < 64, 0.0, dq).astype(bf16)

    @pl.when(k > ids[2])
    def _():
        dkv_out[...] = arrived[...]


def feed_grad_kernel(ids, feed, units, hidden, *refs):
    out, cot = refs[8:]
    span_rows(ids, 0, refs[:8], cot)
    out[:, :512] = dot_tn(feed[...], hidden[...]).astype(bf16)
    out[:, 512:] = dot_tn(cot[...], units[...]).astype(bf16)


def early_grad_kernel(ids, normed, grad, mix, feed_part, vector, *refs):
    out, mixed = refs[4:]
    span_rows(ids, 0, refs[:4], mixed)
    made = dot_tn(normed[...], grad[...])
    both = jnp.where(iota((8, GRAD_ROWS), 0) == 0, feed_part[...], 0.0)
    columns = pltpu.roll(columns_of([both]), 89, 1) + vector[...]
    out[:, :384] = made[:, :384].astype(bf16)
    out[:, 384:512] = (made[:, 384:512] + columns).astype(bf16)
    out[:, 512:768] = made[:, 512:].astype(bf16)
    out[:, 768:] = dot_tn(mixed[...], mix[...]).astype(bf16)


def attend_grad_kernel(ids, normed_ref, gq, gkv_ref, weights, gains, gain_ref, out):
    normed = normed_ref[...]
    lane = iota((SPAN, 128), 1)
    gkv = gkv_ref[...].astype(f32)
    turned = pltpu.roll(gkv, 64, 1)
    first = ids[1] // (ATT_HEADS // KV_HEADS) == 0
    low_lanes = lane < 64
    place = jnp.where(first, low_lanes.astype(jnp.int32), 1 - low_lanes.astype(jnp.int32)) == 1
    keys = jnp.where(place, jnp.where(first, gkv, turned), 0.0)
    vals = jnp.where(place, jnp.where(first, turned, gkv), 0.0)
    both = jnp.concatenate([keys, vals], axis=1).astype(bf16)
    made = dot_tn(normed, jnp.concatenate([gq[...], both], axis=1))
    normal = normed.astype(f32) / gains[0:1, :]
    gain = jnp.sum(dot_nt(both, weights[...]) * normal, axis=0, keepdims=True) + gain_ref[0:1, :]
    gain = jnp.where(iota((8, GRAD_ROWS), 0) == 0, gain, 0.0)
    out[:, :128] = (made[:, :128] + columns_of([gain])).astype(bf16)
    out[:, 128:] = made[:, 128:].astype(bf16)


def scan_back_kernel(
    ids, x_ref, gy_ref, wr_ref, col_ref, row_ref, state_ref, adjoints, params, ggate_ref,
    grad_out, sums,
    carry,
):
    i = pl.program_id(0)

    @pl.when(i == 0)
    def _():
        carry[...] = combine_states(lambda k: adjoints[k], ids[0], True)
        sums[...] = jnp.zeros_like(sums)

    refs = (x_ref, gy_ref, wr_ref, col_ref, row_ref, state_ref, params, ggate_ref)
    later = carry[...]
    for c in reversed(range(PER)):
        later = scan_back_chunk(ids, c, later, refs, grad_out, sums)
    carry[...] = later


def scan_back_chunk(ids, c, later, refs, grad_out, sums):
    x_ref, gy_ref, wr_ref, col_ref, row_ref, state_ref, params, ggate_ref = refs
    here = slice(c * CHUNK, c * CHUNK + CHUNK)
    columns = col_ref[here, :]
    write, read = wr_ref[here, :128], wr_ref[here, 128:]
    entry = state_ref[c]
    later_low, entry_low = later.astype(bf16), entry.astype(bf16)
    x, gy = x_ref[here, :].astype(f32), gy_ref[here, :]
    gy_low = gy.astype(bf16)
    step = spread(columns, 8)
    cum = spread(columns, 0)
    last = row_ref[0:8, c * CHUNK + CHUNK - 1 : c * CHUNK + CHUNK]
    scaled = x * step
    scaled_low = scaled.astype(bf16)
    left = jnp.exp(spread_last(last) - cum)
    entered = jnp.exp(cum)
    products = dot_nt(write, read)
    causal = iota((CHUNK, CHUNK), 0) <= iota((CHUNK, CHUNK), 1)
    wide_lane = iota((CHUNK, WIDE), 1)
    lane = iota((CHUNK, 128), 1)
    from_later = left * dot_nt(write, later_low)
    u = from_later
    summed = jnp.zeros((CHUNK, CHUNK), f32)
    row_sums = jnp.zeros((8, CHUNK), f32)
    col_sums = jnp.zeros((CHUNK, 128), f32)
    head_row = iota((8, CHUNK), 0)
    for h in range(HEADS):
        mine = wide_lane // 64 == h
        span = row_ref[h : h + 1, here] - columns[:, h : h + 1]
        decay = jnp.exp(jnp.where(causal, span, masked_score))
        gy_part = jnp.where(mine, gy_low, jnp.zeros_like(gy_low))
        u = u + dot((decay * products).astype(bf16), gy_part)
        terms = decay * dot_nt(scaled_low, gy_part)
        summed = summed + terms
        terms = terms * products
        row_sums = row_sums + jnp.where(
            head_row == h, jnp.sum(terms, axis=0, keepdims=True), 0.0
        )
        col_sums = col_sums + jnp.where(lane == h, jnp.sum(terms, axis=1, keepdims=True), 0.0)
    grad_out[here, :256] = (step * u).astype(bf16)
    low = summed.astype(bf16)
    grad_out[here, 512:640] = (dot(low, read) + dot((scaled * left).astype(bf16), later_low)).astype(bf16)
    entered_gy = (gy * entered).astype(bf16)
    grad_out[here, 640:768] = (dot_tn(low, write) + dot(entered_gy, entry_low)).astype(bf16)
    carried_part = gy * (entered * dot_nt(read, entry_low))
    listed = (
        select_sum(carried_part, head_select(0))
        - col_sums
        + select_sum(scaled * from_later, head_select(8))
        + select_sum(x * u, head_select(16))
    ).T
    meet = later * entry
    grown = jnp.exp(last)
    eight = iota((8, 1), 0)
    constant = jnp.zeros((8, 1), f32)
    for h in range(HEADS):
        part = jnp.sum(meet[64 * h : 64 * h + 64], axis=0, keepdims=True)
        constant = constant + jnp.where(eight == h, jnp.sum(part, axis=1, keepdims=True), 0.0)
    tails = listed[8:16]
    grad_log = (
        suffix_sum(row_sums + listed[0:8]) + (prefix_sum(tails) - tails) + grown * constant
    )
    rate = jnp.exp(params[:, 1:2])
    grad_raw = (listed[16:24] - rate * grad_log) * row_ref[16:24, here]
    grad_raw = jnp.where(head_row < HEADS, grad_raw, 0.0)
    log_decay = -rate * row_ref[8:16, here]
    rate_sum = jnp.sum(grad_log * log_decay, axis=1, keepdims=True)
    bias_sum = jnp.sum(grad_raw, axis=1, keepdims=True)
    sums[...] += jnp.where(iota((8, 128), 1) == 0, rate_sum, bias_sum)
    steps = pltpu.roll(columns_of([grad_raw]), 64 + HEADS * ids[1], 1).astype(bf16)
    grad_out[here, 256:384] = ggate_ref[here, :128]
    grad_out[here, 384:512] = jnp.where(lane < 64, ggate_ref[here, 128:], steps)
    return spread_rows([grown[h : h + 1] for h in range(HEADS)]) * later + dot_tn(
        entered_gy, read
    )


def normed_back_kernel(
    ids, early, gq, weights, normed, gains, out_0, out_1, out_2, out_3, gain_out, grad
):
    i = pl.program_id(0)

    @pl.when(i == 0)
    def _():
        gain_out[...] = jnp.zeros_like(gain_out)

    grad[...] = early[...]
    grad[:, 128:256] = jnp.where(iota((CHUNK, 128), 1) < 64, early[:, 128:256], gq[...])
    part = dot_nt(grad[...], weights[...])
    normal = normed[...].astype(f32) / gains[0:1, :]
    gain_out[...] += jnp.broadcast_to(
        jnp.sum(part * normal, axis=0, keepdims=True), gain_out.shape
    )
    by_x(ids, i, part.astype(bf16), (out_0, out_1, out_2, out_3))


def along_x_kernel(ids, part_0, part_1, part_2, part_3, own, beside):
    parts = (part_0, part_1, part_2, part_3)
    own[...] = sum(part[0].astype(f32) for part in parts)
    beside[...] = sum(part[1].astype(f32) for part in parts).astype(bf16)


def input_kernel(
    ids, gkv_ref, weights, own, beside, inp, gains, residual_grad, out
):
    lane = iota((128, 128), 1)
    group = ATT_HEADS // KV_HEADS
    gkv = [
        sum(gkv_ref[h].astype(f32) for h in range(group * n, group * n + group))
        for n in range(KV_HEADS)
    ]
    keys = jnp.where(lane < 64, gkv[0], pltpu.roll(gkv[1], 64, 1))
    vals = jnp.where(lane < 64, pltpu.roll(gkv[0], 64, 1), gkv[1])
    both = jnp.concatenate([keys, vals], axis=1).astype(bf16)
    grad = own[...] + beside[...].astype(f32) + dot_nt(both, weights[...])
    values = inp[...].astype(f32)
    scale = lax.rsqrt(jnp.mean(values * values, axis=1, keepdims=True) + norm_eps)
    normal = values * scale
    w = grad * gains[0:1, :]
    out[...] = residual_grad[...] + scale * (
        w - normal * jnp.mean(w * normal, axis=1, keepdims=True)
    )


def sum_along_x(parts, ids):
    own, D = parts[0].shape[1:]
    return kernel_call(
        along_x_kernel,
        1,
        ids,
        [(part, whole(2, own, D)) for part in parts],
        [(shape(own, D), whole(own, D)), (shape(own, D, kind=bf16), whole(own, D))],
    )


def shards(
    layer_input,
    shared_weight,
    mixer_gain,
    feed_gain,
    branch_weight,
    query_weight,
    mamba_weight,
    attend_weight,
    hidden_weight,
    down_weight,
    rate_log,
    step_bias,
    mamba_gain,
    cotangent,
):
    chip, core, head_index = (lax.axis_index(name) for name in ("chip", "core", "head"))
    ids = jnp.stack([2 * chip + core, head_index, chip, core]).astype(jnp.int32)
    steps = SPAN // ROWS
    D = layer_input.shape[1]
    own = layer_input.shape[0]

    common = jnp.concatenate(
        [
            shared_weight[:, 512:],
            mixer_gain[:, None],
            feed_gain[:, None],
            jnp.zeros((8, 38), bf16),
            shared_weight[:, :512],
        ],
        axis=1,
    )
    common = rows(gather(common, "head"))
    early = jnp.concatenate(
        [
            branch_weight[:, 0],
            query_weight,
            branch_weight[:, 1],
            common,
            mamba_weight,
            attend_weight,
        ],
        axis=1,
    )
    input_beside = beside_y(layer_input)
    input_near, early = lax.optimization_barrier((near_x(layer_input, input_beside), early))
    early_same = gather(early, "chip")
    early_other, span_input, cot_beside = lax.optimization_barrier(
        (
            other_core(early_same),
            relayed(layer_input, input_beside, input_near),
            beside_y(cotangent),
        )
    )
    pair = jnp.stack([early_same[..., 1024:], early_other[..., 1024:]], axis=1)
    pair = jnp.where(core == 0, pair, pair[:, ::-1])
    mix_weights = pair.reshape(D, 256)
    mix_beside = beside_y(mix_weights)
    span_input = [(part, whole(*part.shape)) for part in span_input]
    params = jnp.pad(jnp.stack([step_bias, rate_log], axis=1), ((0, 5), (0, 126)))
    gain_row = jnp.pad(mamba_gain[None], ((0, 0), (0, 64)))
    early_spec = whole(CHIPS, 64, 1280)
    normed, x, gate, wr, q, col, row, local, pack, gains, early = kernel_call(
        project_kernel,
        steps,
        ids,
        span_input
        + [(early_same, early_spec), (early_other, early_spec), (params, whole(8, 128))],
        [
            (shape(SPAN, D, kind=bf16), blocks(ROWS, D)),
            (shape(SPAN, WIDE, kind=bf16), blocks(ROWS, WIDE)),
            (shape(SPAN, WIDE), blocks(ROWS, WIDE)),
            (shape(SPAN, 256, kind=bf16), blocks(ROWS, 256)),
            (shape(SPAN, 128, kind=bf16), blocks(ROWS, 128)),
            (shape(SPAN, 128), blocks(ROWS, 128)),
            (shape(24, SPAN), lanes(24, ROWS)),
            (shape(steps * PER, WIDE, STATE), blocks(PER, WIDE, STATE)),
            (shape(CHIPS, PACK, 128, kind=bf16), whole(CHIPS, PACK, 128)),
            (shape(8, D), whole(8, D)),
            (shape(D, 1024, kind=bf16), whole(D, 1024)),
        ],
        [
            pltpu.VMEM((WIDE, STATE), f32),
            pltpu.VMEM((8, 128), f32),
            pltpu.VMEM((ROWS, D), bf16),
        ],
        flops=2 * SPAN * D * 1024,
    )
    pack, mix_beside, cot_near = lax.optimization_barrier(
        (pack, mix_beside, near_x(cotangent, cot_beside))
    )
    same = exchange(pack, "chip")
    same, span_cot = lax.optimization_barrier(
        (same, relayed(cotangent, cot_beside, cot_near))
    )
    mix_near = near_x(mix_weights, mix_beside)
    late = jnp.concatenate([hidden_weight.reshape(-1, 512), down_weight], axis=1)
    late, same = lax.optimization_barrier((late, same))
    late = lax.all_gather(late, SEQ, axis=0, tiled=True)
    other = other_core(same)

    kv_spec = pl.BlockSpec((1, SPAN, 128), lambda i, ids: (jnp.minimum(i, ids[2]), 0, 0))
    peak_state = shape(8, SPAN), whole(8, SPAN)
    accum_state = shape(128, SPAN), whole(128, SPAN)
    peak, accum = kernel_call(
        attend_same_kernel,
        CHIPS,
        ids,
        [(q, whole(SPAN, 128)), (same, kv_spec)],
        [peak_state, accum_state],
        flops=2 * 2 * SPAN * SPAN * 256 * 5,
    )
    state_spec = pl.BlockSpec((CHIPS, 256, 128), lambda i, ids: (0, 4, 0))
    y, low, entries = kernel_call(
        scan_kernel,
        steps,
        ids,
        [
            (x, blocks(ROWS, WIDE)),
            (gate, blocks(ROWS, WIDE)),
            (wr, blocks(ROWS, 256)),
            (col, blocks(ROWS, 128)),
            (row, lanes(24, ROWS)),
            (local, blocks(PER, WIDE, STATE)),
            (same, state_spec),
            (other, state_spec),
            (gain_row, whole(1, WIDE)),
        ],
        [
            (shape(SPAN, WIDE), blocks(ROWS, WIDE)),
            (shape(SPAN, WIDE, kind=bf16), blocks(ROWS, WIDE)),
            (shape(steps * PER, WIDE, STATE), blocks(PER, WIDE, STATE)),
        ],
        [pltpu.VMEM((WIDE, STATE), f32)],
        flops=2 * SPAN * 256 * 256 * 8,
    )
    peak, low, mix_near = lax.optimization_barrier((peak, low, mix_near))
    mix_weights = relayed(mix_weights, mix_beside, mix_near)
    mix, o_pad, lse = kernel_call(
        attend_other_kernel,
        CHIPS,
        ids,
        [
            (q, whole(SPAN, 128)),
            (other, kv_spec),
            (low, whole(SPAN, WIDE)),
            (peak, whole(8, SPAN)),
            (accum, whole(128, SPAN)),
        ],
        [
            (shape(SPAN, 256, kind=bf16), whole(SPAN, 256)),
            (shape(SPAN, 128), whole(SPAN, 128)),
            (shape(8, SPAN), whole(8, SPAN)),
        ],
        [pltpu.VMEM((8, SPAN), f32), pltpu.VMEM((128, SPAN), f32)],
        flops=2 * 2 * SPAN * SPAN * 256 * 5,
    )
    mix, mix_weights = lax.optimization_barrier((mix, mix_weights))
    mix_weights = [(part, whole(*part.shape)) for part in mix_weights]
    mix_own = exchange(mix.reshape(8, own, 256), "head")
    residual, feed_copies = kernel_call(
        residual_kernel,
        1,
        ids,
        [(mix_own, whole(8, own, 256))]
        + mix_weights
        + [(layer_input, whole(own, D)), (gains, whole(8, D))],
        [
            (shape(own, D), whole(own, D)),
            (shape(8, own, D, kind=bf16), whole(8, own, D)),
        ],
        flops=2 * own * D * 2048,
    )
    feed_copies, late = lax.optimization_barrier((feed_copies, late))
    feed = rows(exchange(feed_copies, "head"))
    pair_out = shape(2, own, D, kind=bf16), whole(2, own, D)
    *feed_parts, back_part, units, grad_hidden = kernel_call(
        feed_kernel,
        SPAN // FEED_ROWS,
        ids,
        [(feed, blocks(FEED_ROWS, D))]
        + [(part, whole(*part.shape)) for part in span_cot]
        + [(late, whole(D, 768))],
        [pair_out] * 4
        + [
            (shape(SPAN, D, kind=bf16), blocks(FEED_ROWS, D)),
            (shape(SPAN, 256, kind=bf16), blocks(FEED_ROWS, 256)),
            (shape(SPAN, 512, kind=bf16), blocks(FEED_ROWS, 512)),
        ],
        [pltpu.VMEM((FEED_ROWS, D), bf16)],
        flops=2 * SPAN * D * (512 + 256) * 2,
    )
    back_own = exchange(back_part.reshape(8, own, D), "head")
    (feed_grad,) = kernel_call(
        feed_grad_kernel,
        D // GRAD_ROWS,
        ids,
        [
            (feed, lanes(SPAN, GRAD_ROWS)),
            (units, whole(SPAN, 256)),
            (grad_hidden, whole(SPAN, 512)),
        ]
        + [(part, lanes(*part.shape[:-1], GRAD_ROWS)) for part in span_cot],
        [(shape(D, 768, kind=bf16), blocks(GRAD_ROWS, 768))],
        [pltpu.VMEM((SPAN, GRAD_ROWS), bf16)],
        flops=2 * SPAN * D * 768,
    )
    back_own, feed_grad = lax.optimization_barrier((back_own, feed_grad))
    feed_grad = lax.psum_scatter(feed_grad, SEQ, scatter_dimension=0, tiled=True).astype(f32)
    grad_residual, mixed_copies, feed_gain_part, mix_grads = kernel_call(
        mixed_kernel,
        1,
        ids,
        [
            (back_own, whole(8, own, D)),
            (residual, whole(own, D)),
            (cotangent, whole(own, D)),
            (gains, whole(8, D)),
        ]
        + mix_weights,
        [
            (shape(own, D), whole(own, D)),
            (shape(own, D, kind=bf16), whole(own, D)),
            (shape(8, D), whole(8, D)),
            (shape(8, own, 256, kind=bf16), whole(8, own, 256)),
        ],
        flops=2 * own * D * 2048,
    )
    grad_mix = rows(exchange(mix_grads, "head"))
    grad_mix, mixed_copies = lax.optimization_barrier((grad_mix, mixed_copies))
    mixed_beside = beside_y(mixed_copies)
    gy, ggate, do_pad, delta, adjoint, gain_sum = kernel_call(
        gate_back_kernel,
        steps,
        ids,
        [
            (grad_mix, backwards(blocks(ROWS, 256), steps)),
            (y, backwards(blocks(ROWS, WIDE), steps)),
            (gate, backwards(blocks(ROWS, WIDE), steps)),
            (gain_row, whole(1, WIDE)),
            (wr, backwards(blocks(ROWS, 256), steps)),
            (col, backwards(blocks(ROWS, 128), steps)),
            (row, backwards(lanes(24, ROWS), steps)),
            (o_pad, backwards(blocks(ROWS, 128), steps)),
            (pack, pl.BlockSpec((1, 256, 128), lambda i, ids: (0, 4, 0))),
        ],
        [
            (shape(SPAN, WIDE), backwards(blocks(ROWS, WIDE), steps)),
            (shape(SPAN, WIDE, kind=bf16), backwards(blocks(ROWS, WIDE), steps)),
            (shape(SPAN, 128, kind=bf16), backwards(blocks(ROWS, 128), steps)),
            (shape(8, SPAN), backwards(lanes(8, ROWS), steps)),
            (shape(SPANS, 208, 128, kind=bf16), whole(SPANS, 208, 128)),
            (shape(8, WIDE), whole(8, WIDE)),
        ],
        [pltpu.VMEM((WIDE, STATE), f32)],
        flops=2 * SPAN * 256 * 256 * 4,
    )
    adjoint, mixed_beside = lax.optimization_barrier((adjoint, mixed_beside))
    mixed_pair = jnp.stack([mixed_copies, mixed_beside])
    span_mixed = along_x([mixed_pair] * 4)
    adjoints = exchange(adjoint, SEQ)
    back_ins = [
        (do_pad, whole(SPAN, 128)),
        (lse, whole(8, SPAN)),
        (delta, whole(8, SPAN)),
    ]
    dkv_shape = shape(CHIPS, SPAN, 128, kind=bf16), blocks(1, SPAN, 128)
    dkv_other, dq = kernel_call(
        attend_back_other_kernel,
        CHIPS,
        ids,
        [(q, whole(SPAN, 128)), (other, kv_spec)] + back_ins,
        [dkv_shape, (shape(128, SPAN), whole(128, SPAN))],
        flops=2 * 5 * SPAN * SPAN * 256 * 5,
    )
    dq, adjoints, span_mixed, feed_parts = lax.optimization_barrier(
        (dq, adjoints, span_mixed, feed_parts)
    )
    feed_parts = along_x(feed_parts)
    dkv_other = other_core(dkv_other)
    early_part, sums = kernel_call(
        scan_back_kernel,
        steps,
        ids,
        [
            (x, backwards(blocks(ROWS, WIDE), steps)),
            (gy, backwards(blocks(ROWS, WIDE), steps)),
            (wr, backwards(blocks(ROWS, 256), steps)),
            (col, backwards(blocks(ROWS, 128), steps)),
            (row, backwards(lanes(24, ROWS), steps)),
            (entries, backwards(blocks(PER, WIDE, STATE), steps)),
            (adjoints, whole(SPANS, 208, 128)),
            (params, whole(8, 128)),
            (ggate, backwards(blocks(ROWS, WIDE), steps)),
        ],
        [
            (shape(SPAN, 768, kind=bf16), backwards(blocks(ROWS, 768), steps)),
            (shape(8, 128), whole(8, 128)),
        ],
        [pltpu.VMEM((WIDE, STATE), f32)],
        flops=2 * SPAN * 256 * 256 * 16,
    )
    vector = jnp.concatenate(
        [gain_sum[0, :192], sums[:HEADS, 0], sums[:HEADS, 1], jnp.zeros((58,), f32)]
    ).reshape(64, 4)
    high = lax.reduce_precision(vector, 8, 7)
    vector = jnp.concatenate([high, vector - high], axis=1)
    vector = jnp.pad(jnp.tile(vector, (GRAD_ROWS // 64, 1)), ((0, 0), (90, 30)))
    (early_grad,) = kernel_call(
        early_grad_kernel,
        D // GRAD_ROWS,
        ids,
        [
            (normed, lanes(SPAN, GRAD_ROWS)),
            (early_part, whole(SPAN, 768)),
            (mix, whole(SPAN, 256)),
            (feed_gain_part, lanes(8, GRAD_ROWS)),
            (vector, whole(GRAD_ROWS, 128)),
        ]
        + [(part, lanes(*part.shape[:-1], GRAD_ROWS)) for part in span_mixed],
        [(shape(D, 1024, kind=bf16), blocks(GRAD_ROWS, 1024))],
        [pltpu.VMEM((SPAN, GRAD_ROWS), bf16)],
        flops=2 * SPAN * D * 1024,
    )
    dq, early_grad = lax.optimization_barrier((dq, early_grad))
    early_grad = jnp.sum(
        exchange(early_grad.reshape(SPANS, -1, 1024), SEQ).astype(f32), axis=0
    )
    dkv_same, gq = kernel_call(
        attend_back_same_kernel,
        CHIPS,
        ids,
        [(q, whole(SPAN, 128)), (same, kv_spec)] + back_ins
        + [(dq, whole(128, SPAN)), (dkv_other, blocks(1, SPAN, 128))],
        [dkv_shape, (shape(SPAN, 128, kind=bf16), whole(SPAN, 128))],
        [pltpu.VMEM((128, SPAN), f32)],
        flops=2 * 5 * SPAN * SPAN * 256 * 5,
    )
    dkv_same, early_grad, feed_grad, feed_parts = lax.optimization_barrier(
        (dkv_same, early_grad, feed_grad, feed_parts)
    )
    dkv_own = exchange(dkv_same, "chip")
    *normed_parts, mixer_gain_part = kernel_call(
        normed_back_kernel,
        SPAN // CHUNK,
        ids,
        [
            (early_part, blocks(CHUNK, 768)),
            (gq, blocks(CHUNK, 128)),
            (early, whole(D, 768)),
            (normed, blocks(CHUNK, D)),
            (gains, whole(8, D)),
        ],
        [pair_out] * 4 + [(shape(8, D), whole(8, D))],
        [pltpu.VMEM((CHUNK, 768), bf16)],
        flops=2 * SPAN * D * 768,
    )
    feed_own, feed_beside = sum_along_x(feed_parts, ids)
    feed_beside = beside_y(feed_beside)
    layer_output = (residual + feed_own + feed_beside.astype(f32)).astype(bf16)
    dkv_own = jnp.sum(dkv_own.astype(f32), axis=0).astype(bf16)
    normed_parts = along_x(normed_parts)
    gkv = exchange(dkv_own.reshape(8, own, 128), "head")
    (attend_grads,) = kernel_call(
        attend_grad_kernel,
        D // GRAD_ROWS,
        ids,
        [
            (normed, lanes(SPAN, GRAD_ROWS)),
            (gq, whole(SPAN, 128)),
            (dkv_own, whole(SPAN, 128)),
            (early, pl.BlockSpec((GRAD_ROWS, 256), lambda i, ids: (i, 3))),
            (gains, lanes(8, GRAD_ROWS)),
            (mixer_gain_part, lanes(8, GRAD_ROWS)),
        ],
        [(shape(D, 384, kind=bf16), blocks(GRAD_ROWS, 384))],
        flops=2 * SPAN * D * 640,
    )
    gkv, attend_grads, normed_parts = lax.optimization_barrier((gkv, attend_grads, normed_parts))
    attend_grads = exchange(attend_grads.reshape(SPANS, -1, 384), SEQ)
    normed_own, normed_beside = sum_along_x(normed_parts, ids)
    normed_beside = beside_y(normed_beside)
    (input_grad,) = kernel_call(
        input_kernel,
        1,
        ids,
        [
            (gkv, whole(8, own, 128)),
            (early, pl.BlockSpec((D, 256), lambda i, ids: (0, 3))),
            (normed_own, whole(own, D)),
            (normed_beside, whole(own, D)),
            (layer_input, whole(own, D)),
            (gains, whole(8, D)),
            (grad_residual, whole(own, D)),
        ],
        [(shape(own, D), whole(own, D))],
        flops=2 * own * D * 256,
    )
    attend_grads = jnp.sum(attend_grads.astype(f32), axis=0)
    common_grad = jnp.concatenate(
        [early_grad[:, 448:472], attend_grads[:, :1], early_grad[:, 473:768], attend_grads[:, 128:]],
        axis=1,
    )
    common_grad = jnp.sum(
        exchange(common_grad.astype(bf16).reshape(8, 8, 576), "head").astype(f32), axis=0
    )
    vector = (early_grad[:, 474:478] + early_grad[:, 478:482]).reshape(256)
    return (
        layer_output,
        input_grad,
        jnp.concatenate([common_grad[:, 64:], common_grad[:, :24]], axis=1),
        common_grad[:, 24],
        common_grad[:, 25],
        jnp.stack([early_grad[:, :192], early_grad[:, 256:448]], axis=1),
        attend_grads[:, 64:128],
        early_grad[:, 768:960],
        early_grad[:, 960:],
        feed_grad[:, :512].reshape(-1, 2, 256),
        feed_grad[:, 512:],
        vector[192:195],
        vector[195:198],
        vector[:192],
    )


def solution(mesh):
    devices = mesh.devices.reshape(CHIPS, 2, mesh.shape["head"])
    every = (*SEQ, "head")
    return jax.shard_map(
        shards,
        mesh=jax.sharding.Mesh(devices, every),
        in_specs=(
            P(every, None),
            P(every, None),
            P(every),
            P(every),
            P(SEQ, None, "head"),
            P(SEQ, "head"),
            P(SEQ, "head"),
            P(SEQ, "head"),
            P(SEQ, None, "head"),
            P(SEQ, "head"),
            P("head"),
            P("head"),
            P("head"),
            P(every, None),
        ),
        out_specs=(
            P(every, None),
            P(every, None),
            P(every, None),
            P(every),
            P(every),
            P(SEQ, None, "head"),
            P(SEQ, "head"),
            P(SEQ, "head"),
            P(SEQ, "head"),
            P(SEQ, None, "head"),
            P(SEQ, "head"),
            P("head"),
            P("head"),
            P("head"),
        ),
        check_vma=False,
    )
```

```python
import jax
import jax.numpy as jnp
from jax import lax
from jax.experimental import pallas as pl
from jax.experimental.pallas import tpu as pltpu
from jax.sharding import PartitionSpec as P

HEAD_DIM = 64
STATE = 128
ATT_HEADS = 8
KV_HEADS = 2
HEADS = 3
SPAN = 1024
GRAD_ROWS = 512
FEED_ROWS = 512
KEYS = 512
BACK_KEYS = 256
PER = 2
ROWS = 512
CHUNK = 256
SPANS = 16
CHIPS = 8
SEQ = ("chip", "core")
WIDE = 256
PACK = 1280

norm_eps = 1e-05
masked_score = -1e30
f32, bf16 = jnp.float32, jnp.bfloat16
MIB = 1024 * 1024


def gather(part, axis):
    size = lax.axis_size(axis)
    return lax.all_to_all(jnp.broadcast_to(part[None], (size,) + part.shape), axis, 0, 0)


def beside_y(part):
    return lax.ppermute(part, "head", [(k, k ^ 1) for k in range(8)])


def along_x(pairs):
    return [pairs[0]] + [
        lax.ppermute(pairs[d], "head", [(k, (k + 2 * d) % 8) for k in range(8)])
        for d in (1, 2, 3)
    ]


def shift_x(part, distance):
    return lax.ppermute(part, "head", [(k, (k + 2 * distance) % 8) for k in range(8)])


def near_x(own, beside):
    return [shift_x(own, 1), shift_x(beside, 1), shift_x(own, 3), shift_x(beside, 3)]


def relayed(own, beside, near):
    far = [shift_x(near[0], 1), shift_x(near[3], 3)]
    return [own, beside, *near[:2], *far, *near[2:]]


def other_core(part):
    return lax.ppermute(part, "core", [(0, 1), (1, 0)])


def exchange(pieces, axis):
    return lax.all_to_all(pieces, axis, 0, 0)


def rows(stacked):
    return stacked.reshape((-1,) + stacked.shape[2:])


def whole(*shape):
    return pl.BlockSpec(shape, lambda i, ids: (0,) * len(shape))


def blocks(*shape):
    return pl.BlockSpec(shape, lambda i, ids: (i,) + (0,) * (len(shape) - 1))


def lanes(*shape):
    return pl.BlockSpec(shape, lambda i, ids: (0,) * (len(shape) - 1) + (i,))


def backwards(spec, steps):
    index = spec.index_map
    return pl.BlockSpec(spec.block_shape, lambda i, ids: index(steps - 1 - i, ids))


def kernel_call(body, grid, ids, ins, outs, scratch=(), flops=0, limit=60):
    arrays, in_specs = zip(*ins)
    shapes, out_specs = zip(*outs)
    moved = sum(a.size * a.dtype.itemsize for a in arrays) + sum(
        s.size * s.dtype.itemsize for s in shapes
    )
    return pl.pallas_call(
        body,
        grid_spec=pltpu.PrefetchScalarGridSpec(
            num_scalar_prefetch=1,
            grid=(grid,),
            in_specs=list(in_specs),
            out_specs=list(out_specs),
            scratch_shapes=list(scratch),
        ),
        out_shape=list(shapes),
        compiler_params=pltpu.CompilerParams(
            dimension_semantics=("arbitrary",), vmem_limit_bytes=limit * MIB
        ),
        cost_estimate=pl.CostEstimate(flops=flops, bytes_accessed=moved, transcendentals=0),
    )(ids, *arrays)


def shape(*dims, kind=f32):
    return jax.ShapeDtypeStruct(dims, kind)


def dot(a, b):
    return jnp.dot(a, b, preferred_element_type=f32)


def dot_nt(a, b):
    return lax.dot_general(a, b, (((1,), (1,)), ((), ())), preferred_element_type=f32)


def dot_tn(a, b):
    return lax.dot_general(a, b, (((0,), (0,)), ((), ())), preferred_element_type=f32)


def select_sum(a, b):
    high = a.astype(bf16)
    return dot(high, b) + dot((a - high.astype(f32)).astype(bf16), b)


def iota(dims, axis):
    return lax.broadcasted_iota(jnp.int32, dims, axis)


def spread(columns, base):
    lane = iota((columns.shape[0], WIDE), 1)
    c = [columns[:, base + h : base + h + 1] for h in range(HEADS)]
    return jnp.where(
        lane < 64, c[0], jnp.where(lane < 128, c[1], jnp.where(lane < 192, c[2], 0.0))
    )


def spread_rows(parts):
    row = iota((WIDE, STATE), 0)
    return jnp.where(
        row < 64, parts[0], jnp.where(row < 128, parts[1], jnp.where(row < 192, parts[2], 0.0))
    )


def head_select(offset):
    lane, column = iota((WIDE, 128), 0), iota((WIDE, 128), 1)
    return jnp.where((column == offset + lane // 64) & (lane < 192), 1.0, 0.0).astype(bf16)


def head_mean(values):
    a, b = iota((WIDE, WIDE), 0), iota((WIDE, WIDE), 1)
    return select_sum(values, jnp.where(a // 64 == b // 64, 1.0 / 64, 0.0).astype(bf16))


def prefix_sum(values):
    width = values.shape[1]
    lane = iota(values.shape, 1)
    step = 1
    while step < width:
        values = values + jnp.where(lane >= step, pltpu.roll(values, step, 1), 0.0)
        step *= 2
    return values


def suffix_sum(values):
    width = values.shape[1]
    lane = iota(values.shape, 1)
    step = 1
    while step < width:
        values = values + jnp.where(lane < width - step, pltpu.roll(values, width - step, 1), 0.0)
        step *= 2
    return values


def columns_of(parts):
    n = parts[0].shape[1]
    full = jnp.concatenate(list(parts) + [jnp.zeros((128 - 8 * len(parts), n), f32)], axis=0)
    return full.T


def by_distance(refs):
    if len(refs) == 8:
        return list(zip(refs[0::2], refs[1::2]))
    return [(ref.at[0], ref.at[1]) for ref in refs]


def span_rows(ids, first, refs, tokens):
    head = ids[1]
    beside = lax.rem(head, 2)
    for n in range(tokens.shape[0] // 256):
        distance = lax.rem(head // 2 - (first + n) + 4, 4)
        mine = pl.multiple_of(256 * n + 128 * beside, 128)
        theirs = pl.multiple_of(256 * n + 128 - 128 * beside, 128)
        for d, pair in enumerate(by_distance(refs)):

            @pl.when(distance == d)
            def _(pair=pair, mine=mine, theirs=theirs):
                tokens[pl.ds(mine, 128), :] = pair[0][...]
                tokens[pl.ds(theirs, 128), :] = pair[1][...]


def project_kernel(ids, *refs):
    inputs, (same, other, params) = refs[:8], refs[8:11]
    normed, x_out, gate_out, wr_out, q_out, col_out, row_out = refs[11:18]
    states, pack, gains, weights, carry, total, tokens = refs[18:]
    i = pl.program_id(0)
    head = ids[1]
    kv_head = head // (ATT_HEADS // KV_HEADS)

    @pl.when(i == 0)
    def _():
        carry[...] = jnp.zeros_like(carry)
        total[...] = jnp.zeros_like(total)
        for c in range(CHIPS):
            for part, core in ((same, ids[3]), (other, 1 - ids[3])):
                first = pl.multiple_of((2 * c + core) * 64, 64)
                weights[pl.ds(first, 64), :] = part[c, :, :1024]
        gains[...] = weights[:, 384:512].astype(f32).T[88:96]
        for c in range(CHIPS):
            pack[c, SPAN:, :] = jnp.zeros((PACK - SPAN, 128), bf16)

    span_rows(ids, PER * i, inputs, tokens)
    values = tokens[...].astype(f32)
    scale = lax.rsqrt(jnp.mean(values * values, axis=1, keepdims=True) + norm_eps)
    low = (values * scale * gains[0:1, :]).astype(bf16)
    normed[...] = low
    made = dot(low, weights[...])
    wide_lane = iota((ROWS, WIDE), 1)
    lane = iota((ROWS, 128), 1)
    x = jnp.where(wide_lane < 192, made[:, :256], 0.0).astype(bf16)
    x_out[...] = x
    gate_out[...] = jnp.where(wide_lane < 192, made[:, 256:512], 0.0)
    q = pltpu.roll(made[:, 128:256], 64, 1)
    q_out[...] = jnp.where(lane < 64, q.astype(bf16).astype(f32) * HEAD_DIM**-0.5, 0.0).astype(bf16)
    write = made[:, 512:640].astype(bf16)
    wr_out[:, :128] = write
    wr_out[:, 128:] = made[:, 640:768].astype(bf16)
    keys, vals = made[:, 768:896], made[:, 896:1024]
    first = kv_head == 0
    keys = jnp.where(first, keys, pltpu.roll(keys, 64, 1))
    vals = jnp.where(first, pltpu.roll(vals, 64, 1), vals)
    kv = jnp.where(lane < 64, keys, vals).astype(bf16)
    for c in range(CHIPS):
        pack[c, pl.ds(pl.multiple_of(i * ROWS, ROWS), ROWS), :] = kv

    misc = made[:, 384:512].astype(bf16).astype(f32)
    raws = pltpu.roll(misc, 64 - HEADS * head, 1).T[:8]
    own = iota((8, ROWS), 0) < HEADS
    z = jnp.where(own, raws, 0.0) + params[:, 0:1]
    step = jnp.where(own, jnp.log1p(jnp.exp(-jnp.abs(z))) + jnp.maximum(z, 0.0), 0.0)
    log_decay = -jnp.exp(params[:, 1:2]) * step
    row_out[8:16, :] = step
    row_out[16:24, :] = lax.logistic(z)
    parts = []
    for c in range(PER):
        here = slice(c * CHUNK, c * CHUNK + CHUNK)
        cum = prefix_sum(log_decay[:, here])
        row_out[0:8, here] = cum
        columns = columns_of([cum, step[:, here]])
        col_out[here, :] = columns
        last = cum[:, CHUNK - 1 : CHUNK]
        tail = jnp.exp(spread_last(last) - spread(columns, 0)) * spread(columns, 8)
        fresh = dot_tn((x[here].astype(f32) * tail).astype(bf16), write[here])
        parts.append((last, fresh))
    state, passed = carry[...], total[...]
    for c, (last, fresh) in enumerate(parts):
        states[c] = state
        grown = jnp.exp(last)
        state = spread_rows([grown[h : h + 1] for h in range(HEADS)]) * state + fresh
        passed = passed + jnp.broadcast_to(last, (8, 128))
    carry[...] = state
    total[...] = passed

    @pl.when(i == pl.num_programs(0) - 1)
    def _():
        state = carry[:192].astype(bf16)
        high = total[...].astype(bf16).astype(f32)
        decays = jnp.concatenate([high, total[...] - high], axis=0).astype(bf16)
        for c in range(CHIPS):
            pack[c, SPAN : SPAN + 192, :] = state
            pack[c, SPAN + 192 : SPAN + 208, :] = decays


def spread_last(last):
    lane = iota((1, WIDE), 1)
    return jnp.where(
        lane < 64,
        last[0:1],
        jnp.where(lane < 128, last[1:2], jnp.where(lane < 192, last[2:3], 0.0)),
    )


def combine_states(span_of, place, later):
    passed = jnp.zeros((8, 128), f32)
    entry = jnp.zeros((192, 128), f32)
    row = iota((192, 128), 0)
    order = range(SPANS) if later else reversed(range(SPANS))
    for k in order:
        use = (k > place) if later else (k < place)
        weight = jnp.where(use, jnp.exp(passed), 0.0)
        weights = jnp.where(
            row < 64, weight[0:1], jnp.where(row < 128, weight[1:2], weight[2:3])
        )
        span = span_of(k).astype(f32)
        entry = entry + weights * span[0:192]
        decay = span[192:200] + span[200:208]
        passed = passed + jnp.where(use, decay, 0.0)
    return jnp.concatenate([entry, jnp.zeros((64, 128), f32)], axis=0)


def scan_kernel(
    ids, x_ref, gate_ref, wr_ref, col_ref, row_ref, local, same, other, gain,
    y_out, low_out, state_out,
    carried,
):
    i = pl.program_id(0)

    @pl.when(i == 0)
    def _():
        carried[...] = combine_states(
            lambda k: jnp.where(ids[3] == k % 2, same[k // 2, :208], other[k // 2, :208]),
            ids[0],
            False,
        )

    passed = carried[...]
    entries = []
    for c in range(PER):
        entries.append(local[c] + passed)
        grown = jnp.exp(row_ref[0:8, c * CHUNK + CHUNK - 1 : c * CHUNK + CHUNK])
        passed = spread_rows([grown[h : h + 1] for h in range(HEADS)]) * passed
    carried[...] = passed
    causal = iota((CHUNK, CHUNK), 0) >= iota((CHUNK, CHUNK), 1)
    wide_lane = iota((CHUNK, WIDE), 1)
    for c, entry in enumerate(entries):
        here = slice(c * CHUNK, c * CHUNK + CHUNK)
        state_out[c] = entry
        columns = col_ref[here, :]
        write, read = wr_ref[here, :128], wr_ref[here, 128:]
        cum = spread(columns, 0)
        scaled = (x_ref[here, :].astype(f32) * spread(columns, 8)).astype(bf16)
        products = dot_nt(read, write)
        y = jnp.exp(cum) * dot_nt(read, entry.astype(bf16))
        for h in range(HEADS):
            span = columns[:, h : h + 1] - row_ref[h : h + 1, here]
            weights = jnp.exp(jnp.where(causal, span, masked_score)) * products
            part = jnp.where(wide_lane // 64 == h, scaled, jnp.zeros_like(scaled))
            y = y + dot(weights.astype(bf16), part)
        y_out[here, :] = y
        gate = gate_ref[here, :]
        gated = y * (gate * lax.logistic(gate))
        low = gated * lax.rsqrt(head_mean(gated * gated) + norm_eps) * gain[...]
        low_out[here, :] = low.astype(bf16)


def attend_visit(kv_ref, q_ref, peak, accum, masked):
    before = now = peak[0:1, :]
    blocks_of = []
    for first in range(0, SPAN, KEYS):
        kv = kv_ref[0, first : first + KEYS, :]
        scores = dot_nt(kv, q_ref[...])
        if masked:
            dims = (KEYS, SPAN)
            scores = jnp.where(iota(dims, 0) + first > iota(dims, 1), masked_score, scores)
        now = jnp.maximum(now, jnp.max(scores, axis=0, keepdims=True))
        blocks_of.append((kv, scores))
    total = accum[...] * jnp.exp(before - now)
    for kv, scores in blocks_of:
        ones = jnp.where(iota(kv.shape, 1) < 64, jnp.ones_like(kv), kv)
        total = total + dot_tn(ones, jnp.exp(scores - now).astype(bf16))
    accum[...] = total
    peak[...] = jnp.broadcast_to(now, peak.shape)


def attend_same_kernel(ids, q_ref, kv_ref, peak, accum):
    k = pl.program_id(0)

    @pl.when(k == 0)
    def _():
        peak[...] = jnp.full_like(peak, masked_score)
        accum[...] = jnp.zeros_like(accum)

    @pl.when(k < ids[2])
    def _():
        attend_visit(kv_ref, q_ref, peak, accum, False)

    @pl.when(k == ids[2])
    def _():
        attend_visit(kv_ref, q_ref, peak, accum, True)


def attend_other_kernel(
    ids, q_ref, kv_ref, low_ref, peak_in, accum_in, mix_out, o_out, lse_out, peak, accum
):
    k = pl.program_id(0)

    @pl.when(k == 0)
    def _():
        peak[...] = peak_in[...]
        accum[...] = accum_in[...]

    @pl.when(k < ids[2] + ids[3])
    def _():
        attend_visit(kv_ref, q_ref, peak, accum, False)

    @pl.when(k == pl.num_programs(0) - 1)
    def _():
        lane = iota((SPAN, 128), 1)
        total = accum[0:1, :]
        out = (accum[...] / total).T
        o_out[...] = out
        mix_out[:, :128] = low_ref[:, :128]
        mix_out[:, 128:] = jnp.where(lane < 64, low_ref[:, 128:], out.astype(bf16))
        lse_out[...] = peak[...] + jnp.log(total)


def by_head(ids, refs):
    head = ids[1]
    for d, pair in enumerate(by_distance(refs)):
        x = lax.rem(head // 2 - d + 4, 4)
        for t in range(2):
            yield 2 * x + lax.rem(head + t, 2), pair[t]


def residual_kernel(ids, mix, *refs):
    weight_refs, (inp, gains, residual_out, feed_out) = refs[:8], refs[8:]
    total = jnp.zeros(residual_out.shape, f32)
    for h, weights in by_head(ids, weight_refs):
        total = total + dot_nt(mix[h], weights[...])
    residual = inp[...].astype(f32) + total
    residual_out[...] = residual
    scale = lax.rsqrt(jnp.mean(residual * residual, axis=1, keepdims=True) + norm_eps)
    feed = (residual * scale * gains[1:2, :]).astype(bf16)
    for h in range(8):
        feed_out[h] = feed


def by_x(ids, first, part, outs):
    beside = lax.rem(ids[1], 2)
    for n in range(part.shape[0] // 256):
        distance = lax.rem(first + n - ids[1] // 2 + 4, 4)
        for d, out in enumerate(outs):

            @pl.when(distance == d)
            def _(out=out, n=n):
                out[beside] = part[256 * n : 256 * n + 128]
                out[1 - beside] = part[256 * n + 128 : 256 * n + 256]


def feed_kernel(ids, feed, *refs):
    weights, *parts, back_out, units_out, hidden_out, cot = refs[8:]
    first = pl.program_id(0) * (FEED_ROWS // 256)
    span_rows(ids, first, refs[:8], cot)
    hidden = dot(feed[...], weights[:, :512])
    gate, up = hidden[:, :256], hidden[:, 256:]
    sig = lax.logistic(gate)
    swish = gate * sig
    units = (swish * up).astype(bf16)
    units_out[...] = units
    down = weights[:, 512:768]
    part = dot_nt(units, down).astype(bf16)
    by_x(ids, first, part, parts)
    grad_units = dot(cot[...], down)
    grad_gate = grad_units * up * (sig * (1.0 + gate * (1.0 - sig)))
    grad_hidden = jnp.concatenate([grad_gate, grad_units * swish], axis=1).astype(bf16)
    hidden_out[...] = grad_hidden
    back_out[...] = dot_nt(grad_hidden, weights[:, :512]).astype(bf16)


def mixed_kernel(ids, back, residual_ref, cot, gains, *refs):
    weight_refs, (grad_out, copies, gain_out, parts) = refs[:8], refs[8:]
    grad_feed = back[0].astype(f32)
    for h in range(1, 8):
        grad_feed = grad_feed + back[h].astype(f32)
    residual = residual_ref[...]
    scale = lax.rsqrt(jnp.mean(residual * residual, axis=1, keepdims=True) + norm_eps)
    normal = residual * scale
    gain_out[...] = jnp.broadcast_to(
        jnp.sum(grad_feed * normal, axis=0, keepdims=True), gain_out.shape
    )
    w = grad_feed * gains[1:2, :]
    grad = cot[...].astype(f32) + scale * (
        w - normal * jnp.mean(w * normal, axis=1, keepdims=True)
    )
    grad_out[...] = grad
    low = grad.astype(bf16)
    copies[...] = low
    for h, weights in by_head(ids, weight_refs):
        parts[h] = dot(low, weights[...]).astype(bf16)


def gate_back_kernel(
    ids, grad_ref, y_ref, gate_ref, gain, wr_ref, col_ref, row_ref, o_ref, decays,
    gy_out, ggate_out, do_out, delta_out, pack, gain_out,
    carry,
):
    i = pl.program_id(0)

    @pl.when(i == 0)
    def _():
        carry[...] = jnp.zeros_like(carry)
        gain_out[...] = jnp.zeros_like(gain_out)

    wide_lane = iota((ROWS, WIDE), 1)
    lane = iota((ROWS, 128), 1)
    own = wide_lane < 192
    grad_all = grad_ref[...].astype(f32)
    grad = jnp.where(own, grad_all, 0.0)
    grad_out = jnp.where(lane < 64, 0.0, grad_all[:, 128:])
    do_out[...] = grad_out.astype(bf16)
    delta = jnp.sum((grad_out * o_ref[...]).T, axis=0, keepdims=True)
    delta_out[...] = jnp.broadcast_to(delta, (8, ROWS))
    y, gate = y_ref[...], gate_ref[...]
    sig = lax.logistic(gate)
    swish = gate * sig
    m = y * swish
    q = lax.rsqrt(head_mean(m * m) + norm_eps)
    gain_out[...] += jnp.broadcast_to(jnp.sum(grad * m * q, axis=0, keepdims=True), (8, WIDE))
    w = grad * gain[...]
    grad_gated = q * (w - m * (q * q) * head_mean(w * m))
    gy = grad_gated * swish
    gy_out[...] = gy
    ggate_out[...] = (grad_gated * y * (sig * (1.0 + gate * (1.0 - sig)))).astype(bf16)
    weighted = (gy * jnp.exp(spread(col_ref[...], 0))).astype(bf16)
    state = carry[...]
    for c in reversed(range(PER)):
        here = slice(c * CHUNK, c * CHUNK + CHUNK)
        grown = jnp.exp(row_ref[0:8, c * CHUNK + CHUNK - 1 : c * CHUNK + CHUNK])
        state = spread_rows([grown[h : h + 1] for h in range(HEADS)]) * state + dot_tn(
            weighted[here], wr_ref[here, 128:]
        )
    carry[...] = state

    @pl.when(i == pl.num_programs(0) - 1)
    def _():
        state = carry[:192].astype(bf16)
        for c in range(SPANS):
            pack[c, :192, :] = state
            pack[c, 192:208, :] = decays[0, 192:208, :]


def attend_back_visit(refs, masked, arrived=None):
    q_ref, kv_ref, do_ref, lse, delta, dkv_out, accum = refs
    for first in range(0, SPAN, BACK_KEYS):
        here = slice(first, first + BACK_KEYS)
        kv = kv_ref[0, here, :]
        scores = dot_nt(kv, q_ref[...])
        if masked:
            dims = (BACK_KEYS, SPAN)
            scores = jnp.where(iota(dims, 0) + first > iota(dims, 1), masked_score, scores)
        probs = jnp.exp(scores - lse[0:1, :])
        grad_probs = dot_nt(kv, do_ref[...])
        grad_scores = (probs * (grad_probs - delta[0:1, :])).astype(bf16)
        dkv = dot(probs.astype(bf16), do_ref[...]) + dot(grad_scores, q_ref[...])
        if arrived is not None:
            dkv = dkv + arrived[0, here, :].astype(f32)
        dkv_out[0, here, :] = dkv.astype(bf16)
        accum[...] += dot_tn(kv, grad_scores)


def attend_back_other_kernel(ids, q_ref, kv_ref, do_ref, lse, delta, dkv_out, dq_out):
    k = pl.program_id(0)
    seen = ids[2] + ids[3]

    @pl.when(k == 0)
    def _():
        dq_out[...] = jnp.zeros_like(dq_out)

    @pl.when(k < seen)
    def _():
        attend_back_visit((q_ref, kv_ref, do_ref, lse, delta, dkv_out, dq_out), False)

    @pl.when(k >= seen)
    def _():
        dkv_out[...] = jnp.zeros_like(dkv_out)


def attend_back_same_kernel(
    ids, q_ref, kv_ref, do_ref, lse, delta, dq_in, arrived, dkv_out, dq_out, accum
):
    k = pl.program_id(0)
    refs = (q_ref, kv_ref, do_ref, lse, delta, dkv_out, accum)

    @pl.when(k == 0)
    def _():
        accum[...] = dq_in[...]

    @pl.when(k < ids[2])
    def _():
        attend_back_visit(refs, False, arrived)

    @pl.when(k == ids[2])
    def _():
        attend_back_visit(refs, True, arrived)
        dq = pltpu.roll((accum[...] * HEAD_DIM**-0.5).T, 64, 1)
        dq_out[...] = jnp.where(iota((SPAN, 128), 1) < 64, 0.0, dq).astype(bf16)

    @pl.when(k > ids[2])
    def _():
        dkv_out[...] = arrived[...]


def feed_grad_kernel(ids, feed, units, hidden, *refs):
    out, cot = refs[8:]
    span_rows(ids, 0, refs[:8], cot)
    out[:, :512] = dot_tn(feed[...], hidden[...]).astype(bf16)
    out[:, 512:] = dot_tn(cot[...], units[...]).astype(bf16)


def early_grad_kernel(ids, normed, grad, mix, feed_part, vector, *refs):
    out, mixed = refs[4:]
    span_rows(ids, 0, refs[:4], mixed)
    made = dot_tn(normed[...], grad[...])
    both = jnp.where(iota((8, GRAD_ROWS), 0) == 0, feed_part[...], 0.0)
    columns = pltpu.roll(columns_of([both]), 89, 1) + vector[...]
    out[:, :384] = made[:, :384].astype(bf16)
    out[:, 384:512] = (made[:, 384:512] + columns).astype(bf16)
    out[:, 512:768] = made[:, 512:].astype(bf16)
    out[:, 768:] = dot_tn(mixed[...], mix[...]).astype(bf16)


def attend_grad_kernel(ids, normed_ref, gq, gkv_ref, weights, gains, gain_ref, out):
    normed = normed_ref[...]
    lane = iota((SPAN, 128), 1)
    gkv = gkv_ref[...].astype(f32)
    turned = pltpu.roll(gkv, 64, 1)
    first = ids[1] // (ATT_HEADS // KV_HEADS) == 0
    low_lanes = lane < 64
    place = jnp.where(first, low_lanes.astype(jnp.int32), 1 - low_lanes.astype(jnp.int32)) == 1
    keys = jnp.where(place, jnp.where(first, gkv, turned), 0.0)
    vals = jnp.where(place, jnp.where(first, turned, gkv), 0.0)
    both = jnp.concatenate([keys, vals], axis=1).astype(bf16)
    made = dot_tn(normed, jnp.concatenate([gq[...], both], axis=1))
    normal = normed.astype(f32) / gains[0:1, :]
    gain = jnp.sum(dot_nt(both, weights[...]) * normal, axis=0, keepdims=True) + gain_ref[0:1, :]
    gain = jnp.where(iota((8, GRAD_ROWS), 0) == 0, gain, 0.0)
    out[:, :128] = (made[:, :128] + columns_of([gain])).astype(bf16)
    out[:, 128:] = made[:, 128:].astype(bf16)


def scan_back_kernel(
    ids, x_ref, gy_ref, wr_ref, col_ref, row_ref, state_ref, adjoints, params, ggate_ref,
    grad_out, sums,
    carry,
):
    i = pl.program_id(0)

    @pl.when(i == 0)
    def _():
        carry[...] = combine_states(lambda k: adjoints[k], ids[0], True)
        sums[...] = jnp.zeros_like(sums)

    refs = (x_ref, gy_ref, wr_ref, col_ref, row_ref, state_ref, params, ggate_ref)
    later = carry[...]
    for c in reversed(range(PER)):
        later = scan_back_chunk(ids, c, later, refs, grad_out, sums)
    carry[...] = later


def scan_back_chunk(ids, c, later, refs, grad_out, sums):
    x_ref, gy_ref, wr_ref, col_ref, row_ref, state_ref, params, ggate_ref = refs
    here = slice(c * CHUNK, c * CHUNK + CHUNK)
    columns = col_ref[here, :]
    write, read = wr_ref[here, :128], wr_ref[here, 128:]
    entry = state_ref[c]
    later_low, entry_low = later.astype(bf16), entry.astype(bf16)
    x, gy = x_ref[here, :].astype(f32), gy_ref[here, :]
    gy_low = gy.astype(bf16)
    step = spread(columns, 8)
    cum = spread(columns, 0)
    last = row_ref[0:8, c * CHUNK + CHUNK - 1 : c * CHUNK + CHUNK]
    scaled = x * step
    scaled_low = scaled.astype(bf16)
    left = jnp.exp(spread_last(last) - cum)
    entered = jnp.exp(cum)
    products = dot_nt(write, read)
    causal = iota((CHUNK, CHUNK), 0) <= iota((CHUNK, CHUNK), 1)
    wide_lane = iota((CHUNK, WIDE), 1)
    lane = iota((CHUNK, 128), 1)
    from_later = left * dot_nt(write, later_low)
    u = from_later
    summed = jnp.zeros((CHUNK, CHUNK), f32)
    row_sums = jnp.zeros((8, CHUNK), f32)
    col_sums = jnp.zeros((CHUNK, 128), f32)
    head_row = iota((8, CHUNK), 0)
    for h in range(HEADS):
        mine = wide_lane // 64 == h
        span = row_ref[h : h + 1, here] - columns[:, h : h + 1]
        decay = jnp.exp(jnp.where(causal, span, masked_score))
        gy_part = jnp.where(mine, gy_low, jnp.zeros_like(gy_low))
        u = u + dot((decay * products).astype(bf16), gy_part)
        terms = decay * dot_nt(scaled_low, gy_part)
        summed = summed + terms
        terms = terms * products
        row_sums = row_sums + jnp.where(
            head_row == h, jnp.sum(terms, axis=0, keepdims=True), 0.0
        )
        col_sums = col_sums + jnp.where(lane == h, jnp.sum(terms, axis=1, keepdims=True), 0.0)
    grad_out[here, :256] = (step * u).astype(bf16)
    low = summed.astype(bf16)
    grad_out[here, 512:640] = (dot(low, read) + dot((scaled * left).astype(bf16), later_low)).astype(bf16)
    entered_gy = (gy * entered).astype(bf16)
    grad_out[here, 640:768] = (dot_tn(low, write) + dot(entered_gy, entry_low)).astype(bf16)
    carried_part = gy * (entered * dot_nt(read, entry_low))
    listed = (
        select_sum(carried_part, head_select(0))
        - col_sums
        + select_sum(scaled * from_later, head_select(8))
        + select_sum(x * u, head_select(16))
    ).T
    meet = later * entry
    grown = jnp.exp(last)
    eight = iota((8, 1), 0)
    constant = jnp.zeros((8, 1), f32)
    for h in range(HEADS):
        part = jnp.sum(meet[64 * h : 64 * h + 64], axis=0, keepdims=True)
        constant = constant + jnp.where(eight == h, jnp.sum(part, axis=1, keepdims=True), 0.0)
    tails = listed[8:16]
    grad_log = (
        suffix_sum(row_sums + listed[0:8]) + (prefix_sum(tails) - tails) + grown * constant
    )
    rate = jnp.exp(params[:, 1:2])
    grad_raw = (listed[16:24] - rate * grad_log) * row_ref[16:24, here]
    grad_raw = jnp.where(head_row < HEADS, grad_raw, 0.0)
    log_decay = -rate * row_ref[8:16, here]
    rate_sum = jnp.sum(grad_log * log_decay, axis=1, keepdims=True)
    bias_sum = jnp.sum(grad_raw, axis=1, keepdims=True)
    sums[...] += jnp.where(iota((8, 128), 1) == 0, rate_sum, bias_sum)
    steps = pltpu.roll(columns_of([grad_raw]), 64 + HEADS * ids[1], 1).astype(bf16)
    grad_out[here, 256:384] = ggate_ref[here, :128]
    grad_out[here, 384:512] = jnp.where(lane < 64, ggate_ref[here, 128:], steps)
    return spread_rows([grown[h : h + 1] for h in range(HEADS)]) * later + dot_tn(
        entered_gy, read
    )


def normed_back_kernel(
    ids, early, gq, weights, normed, gains, out_0, out_1, out_2, out_3, gain_out, grad
):
    i = pl.program_id(0)

    @pl.when(i == 0)
    def _():
        gain_out[...] = jnp.zeros_like(gain_out)

    grad[...] = early[...]
    grad[:, 128:256] = jnp.where(iota((CHUNK, 128), 1) < 64, early[:, 128:256], gq[...])
    part = dot_nt(grad[...], weights[...])
    normal = normed[...].astype(f32) / gains[0:1, :]
    gain_out[...] += jnp.broadcast_to(
        jnp.sum(part * normal, axis=0, keepdims=True), gain_out.shape
    )
    by_x(ids, i, part.astype(bf16), (out_0, out_1, out_2, out_3))


def along_x_kernel(ids, part_0, part_1, part_2, part_3, own, beside):
    parts = (part_0, part_1, part_2, part_3)
    own[...] = sum(part[0].astype(f32) for part in parts)
    beside[...] = sum(part[1].astype(f32) for part in parts).astype(bf16)


def input_kernel(
    ids, gkv_ref, weights, own, beside, inp, gains, residual_grad, out
):
    lane = iota((128, 128), 1)
    group = ATT_HEADS // KV_HEADS
    gkv = [
        sum(gkv_ref[h].astype(f32) for h in range(group * n, group * n + group))
        for n in range(KV_HEADS)
    ]
    keys = jnp.where(lane < 64, gkv[0], pltpu.roll(gkv[1], 64, 1))
    vals = jnp.where(lane < 64, pltpu.roll(gkv[0], 64, 1), gkv[1])
    both = jnp.concatenate([keys, vals], axis=1).astype(bf16)
    grad = own[...] + beside[...].astype(f32) + dot_nt(both, weights[...])
    values = inp[...].astype(f32)
    scale = lax.rsqrt(jnp.mean(values * values, axis=1, keepdims=True) + norm_eps)
    normal = values * scale
    w = grad * gains[0:1, :]
    out[...] = residual_grad[...] + scale * (
        w - normal * jnp.mean(w * normal, axis=1, keepdims=True)
    )


def sum_along_x(parts, ids):
    own, D = parts[0].shape[1:]
    return kernel_call(
        along_x_kernel,
        1,
        ids,
        [(part, whole(2, own, D)) for part in parts],
        [(shape(own, D), whole(own, D)), (shape(own, D, kind=bf16), whole(own, D))],
    )


def shards(
    layer_input,
    shared_weight,
    mixer_gain,
    feed_gain,
    branch_weight,
    query_weight,
    mamba_weight,
    attend_weight,
    hidden_weight,
    down_weight,
    rate_log,
    step_bias,
    mamba_gain,
    cotangent,
):
    chip, core, head_index = (lax.axis_index(name) for name in ("chip", "core", "head"))
    ids = jnp.stack([2 * chip + core, head_index, chip, core]).astype(jnp.int32)
    steps = SPAN // ROWS
    D = layer_input.shape[1]
    own = layer_input.shape[0]

    common = jnp.concatenate(
        [
            shared_weight[:, 512:],
            mixer_gain[:, None],
            feed_gain[:, None],
            jnp.zeros((8, 38), bf16),
            shared_weight[:, :512],
        ],
        axis=1,
    )
    common = rows(gather(common, "head"))
    early = jnp.concatenate(
        [
            branch_weight[:, 0],
            query_weight,
            branch_weight[:, 1],
            common,
            mamba_weight,
            attend_weight,
        ],
        axis=1,
    )
    input_beside = beside_y(layer_input)
    input_near, early = lax.optimization_barrier((near_x(layer_input, input_beside), early))
    early_same = gather(early, "chip")
    early_same, span_input, cot_beside = lax.optimization_barrier(
        (early_same, relayed(layer_input, input_beside, input_near), beside_y(cotangent))
    )
    early_other = other_core(early_same)
    pair = jnp.stack([early_same[..., 1024:], early_other[..., 1024:]], axis=1)
    pair = jnp.where(core == 0, pair, pair[:, ::-1])
    mix_weights = pair.reshape(D, 256)
    mix_beside = beside_y(mix_weights)
    span_input = [(part, whole(*part.shape)) for part in span_input]
    params = jnp.pad(jnp.stack([step_bias, rate_log], axis=1), ((0, 5), (0, 126)))
    gain_row = jnp.pad(mamba_gain[None], ((0, 0), (0, 64)))
    early_spec = whole(CHIPS, 64, 1280)
    normed, x, gate, wr, q, col, row, local, pack, gains, early = kernel_call(
        project_kernel,
        steps,
        ids,
        span_input
        + [(early_same, early_spec), (early_other, early_spec), (params, whole(8, 128))],
        [
            (shape(SPAN, D, kind=bf16), blocks(ROWS, D)),
            (shape(SPAN, WIDE, kind=bf16), blocks(ROWS, WIDE)),
            (shape(SPAN, WIDE), blocks(ROWS, WIDE)),
            (shape(SPAN, 256, kind=bf16), blocks(ROWS, 256)),
            (shape(SPAN, 128, kind=bf16), blocks(ROWS, 128)),
            (shape(SPAN, 128), blocks(ROWS, 128)),
            (shape(24, SPAN), lanes(24, ROWS)),
            (shape(steps * PER, WIDE, STATE), blocks(PER, WIDE, STATE)),
            (shape(CHIPS, PACK, 128, kind=bf16), whole(CHIPS, PACK, 128)),
            (shape(8, D), whole(8, D)),
            (shape(D, 1024, kind=bf16), whole(D, 1024)),
        ],
        [
            pltpu.VMEM((WIDE, STATE), f32),
            pltpu.VMEM((8, 128), f32),
            pltpu.VMEM((ROWS, D), bf16),
        ],
        flops=2 * SPAN * D * 1024,
    )
    pack, mix_beside, cotangent_sent = lax.optimization_barrier((pack, mix_beside, cotangent))
    cot_near = near_x(cotangent_sent, cot_beside)
    same = exchange(pack, "chip")
    same, span_cot = lax.optimization_barrier(
        (same, relayed(cotangent, cot_beside, cot_near))
    )
    mix_near = near_x(mix_weights, mix_beside)
    late = jnp.concatenate([hidden_weight.reshape(-1, 512), down_weight], axis=1)
    late, same = lax.optimization_barrier((late, same))
    late = lax.all_gather(late, SEQ, axis=0, tiled=True)
    other = other_core(same)

    kv_spec = pl.BlockSpec((1, SPAN, 128), lambda i, ids: (jnp.minimum(i, ids[2]), 0, 0))
    peak_state = shape(8, SPAN), whole(8, SPAN)
    accum_state = shape(128, SPAN), whole(128, SPAN)
    peak, accum = kernel_call(
        attend_same_kernel,
        CHIPS,
        ids,
        [(q, whole(SPAN, 128)), (same, kv_spec)],
        [peak_state, accum_state],
        flops=2 * 2 * SPAN * SPAN * 256 * 5,
    )
    state_spec = pl.BlockSpec((CHIPS, 256, 128), lambda i, ids: (0, 4, 0))
    y, low, entries = kernel_call(
        scan_kernel,
        steps,
        ids,
        [
            (x, blocks(ROWS, WIDE)),
            (gate, blocks(ROWS, WIDE)),
            (wr, blocks(ROWS, 256)),
            (col, blocks(ROWS, 128)),
            (row, lanes(24, ROWS)),
            (local, blocks(PER, WIDE, STATE)),
            (same, state_spec),
            (other, state_spec),
            (gain_row, whole(1, WIDE)),
        ],
        [
            (shape(SPAN, WIDE), blocks(ROWS, WIDE)),
            (shape(SPAN, WIDE, kind=bf16), blocks(ROWS, WIDE)),
            (shape(steps * PER, WIDE, STATE), blocks(PER, WIDE, STATE)),
        ],
        [pltpu.VMEM((WIDE, STATE), f32)],
        flops=2 * SPAN * 256 * 256 * 8,
    )
    peak, low, mix_near = lax.optimization_barrier((peak, low, mix_near))
    mix_weights = relayed(mix_weights, mix_beside, mix_near)
    mix, o_pad, lse = kernel_call(
        attend_other_kernel,
        CHIPS,
        ids,
        [
            (q, whole(SPAN, 128)),
            (other, kv_spec),
            (low, whole(SPAN, WIDE)),
            (peak, whole(8, SPAN)),
            (accum, whole(128, SPAN)),
        ],
        [
            (shape(SPAN, 256, kind=bf16), whole(SPAN, 256)),
            (shape(SPAN, 128), whole(SPAN, 128)),
            (shape(8, SPAN), whole(8, SPAN)),
        ],
        [pltpu.VMEM((8, SPAN), f32), pltpu.VMEM((128, SPAN), f32)],
        flops=2 * 2 * SPAN * SPAN * 256 * 5,
    )
    mix, mix_weights = lax.optimization_barrier((mix, mix_weights))
    mix_weights = [(part, whole(*part.shape)) for part in mix_weights]
    mix_own = exchange(mix.reshape(8, own, 256), "head")
    residual, feed_copies = kernel_call(
        residual_kernel,
        1,
        ids,
        [(mix_own, whole(8, own, 256))]
        + mix_weights
        + [(layer_input, whole(own, D)), (gains, whole(8, D))],
        [
            (shape(own, D), whole(own, D)),
            (shape(8, own, D, kind=bf16), whole(8, own, D)),
        ],
        flops=2 * own * D * 2048,
    )
    feed_copies, late = lax.optimization_barrier((feed_copies, late))
    feed = rows(exchange(feed_copies, "head"))
    pair_out = shape(2, own, D, kind=bf16), whole(2, own, D)
    *feed_parts, back_part, units, grad_hidden = kernel_call(
        feed_kernel,
        SPAN // FEED_ROWS,
        ids,
        [(feed, blocks(FEED_ROWS, D))]
        + [(part, whole(*part.shape)) for part in span_cot]
        + [(late, whole(D, 768))],
        [pair_out] * 4
        + [
            (shape(SPAN, D, kind=bf16), blocks(FEED_ROWS, D)),
            (shape(SPAN, 256, kind=bf16), blocks(FEED_ROWS, 256)),
            (shape(SPAN, 512, kind=bf16), blocks(FEED_ROWS, 512)),
        ],
        [pltpu.VMEM((FEED_ROWS, D), bf16)],
        flops=2 * SPAN * D * (512 + 256) * 2,
    )
    back_own = exchange(back_part.reshape(8, own, D), "head")
    (feed_grad,) = kernel_call(
        feed_grad_kernel,
        D // GRAD_ROWS,
        ids,
        [
            (feed, lanes(SPAN, GRAD_ROWS)),
            (units, whole(SPAN, 256)),
            (grad_hidden, whole(SPAN, 512)),
        ]
        + [(part, lanes(*part.shape[:-1], GRAD_ROWS)) for part in span_cot],
        [(shape(D, 768, kind=bf16), blocks(GRAD_ROWS, 768))],
        [pltpu.VMEM((SPAN, GRAD_ROWS), bf16)],
        flops=2 * SPAN * D * 768,
    )
    back_own, feed_grad = lax.optimization_barrier((back_own, feed_grad))
    feed_grad = lax.psum_scatter(feed_grad, SEQ, scatter_dimension=0, tiled=True).astype(f32)
    grad_residual, mixed_copies, feed_gain_part, mix_grads = kernel_call(
        mixed_kernel,
        1,
        ids,
        [
            (back_own, whole(8, own, D)),
            (residual, whole(own, D)),
            (cotangent, whole(own, D)),
            (gains, whole(8, D)),
        ]
        + mix_weights,
        [
            (shape(own, D), whole(own, D)),
            (shape(own, D, kind=bf16), whole(own, D)),
            (shape(8, D), whole(8, D)),
            (shape(8, own, 256, kind=bf16), whole(8, own, 256)),
        ],
        flops=2 * own * D * 2048,
    )
    grad_mix = rows(exchange(mix_grads, "head"))
    grad_mix, mixed_copies = lax.optimization_barrier((grad_mix, mixed_copies))
    mixed_beside = beside_y(mixed_copies)
    gy, ggate, do_pad, delta, adjoint, gain_sum = kernel_call(
        gate_back_kernel,
        steps,
        ids,
        [
            (grad_mix, backwards(blocks(ROWS, 256), steps)),
            (y, backwards(blocks(ROWS, WIDE), steps)),
            (gate, backwards(blocks(ROWS, WIDE), steps)),
            (gain_row, whole(1, WIDE)),
            (wr, backwards(blocks(ROWS, 256), steps)),
            (col, backwards(blocks(ROWS, 128), steps)),
            (row, backwards(lanes(24, ROWS), steps)),
            (o_pad, backwards(blocks(ROWS, 128), steps)),
            (pack, pl.BlockSpec((1, 256, 128), lambda i, ids: (0, 4, 0))),
        ],
        [
            (shape(SPAN, WIDE), backwards(blocks(ROWS, WIDE), steps)),
            (shape(SPAN, WIDE, kind=bf16), backwards(blocks(ROWS, WIDE), steps)),
            (shape(SPAN, 128, kind=bf16), backwards(blocks(ROWS, 128), steps)),
            (shape(8, SPAN), backwards(lanes(8, ROWS), steps)),
            (shape(SPANS, 208, 128, kind=bf16), whole(SPANS, 208, 128)),
            (shape(8, WIDE), whole(8, WIDE)),
        ],
        [pltpu.VMEM((WIDE, STATE), f32)],
        flops=2 * SPAN * 256 * 256 * 4,
    )
    adjoint, mixed_beside = lax.optimization_barrier((adjoint, mixed_beside))
    mixed_pair = jnp.stack([mixed_copies, mixed_beside])
    span_mixed = along_x([mixed_pair] * 4)
    adjoints = exchange(adjoint, SEQ)
    back_ins = [
        (do_pad, whole(SPAN, 128)),
        (lse, whole(8, SPAN)),
        (delta, whole(8, SPAN)),
    ]
    dkv_shape = shape(CHIPS, SPAN, 128, kind=bf16), blocks(1, SPAN, 128)
    dkv_other, dq = kernel_call(
        attend_back_other_kernel,
        CHIPS,
        ids,
        [(q, whole(SPAN, 128)), (other, kv_spec)] + back_ins,
        [dkv_shape, (shape(128, SPAN), whole(128, SPAN))],
        flops=2 * 5 * SPAN * SPAN * 256 * 5,
    )
    dq, adjoints, span_mixed, feed_parts = lax.optimization_barrier(
        (dq, adjoints, span_mixed, feed_parts)
    )
    feed_parts = along_x(feed_parts)
    dkv_other = other_core(dkv_other)
    early_part, sums = kernel_call(
        scan_back_kernel,
        steps,
        ids,
        [
            (x, backwards(blocks(ROWS, WIDE), steps)),
            (gy, backwards(blocks(ROWS, WIDE), steps)),
            (wr, backwards(blocks(ROWS, 256), steps)),
            (col, backwards(blocks(ROWS, 128), steps)),
            (row, backwards(lanes(24, ROWS), steps)),
            (entries, backwards(blocks(PER, WIDE, STATE), steps)),
            (adjoints, whole(SPANS, 208, 128)),
            (params, whole(8, 128)),
            (ggate, backwards(blocks(ROWS, WIDE), steps)),
        ],
        [
            (shape(SPAN, 768, kind=bf16), backwards(blocks(ROWS, 768), steps)),
            (shape(8, 128), whole(8, 128)),
        ],
        [pltpu.VMEM((WIDE, STATE), f32)],
        flops=2 * SPAN * 256 * 256 * 16,
    )
    vector = jnp.concatenate(
        [gain_sum[0, :192], sums[:HEADS, 0], sums[:HEADS, 1], jnp.zeros((58,), f32)]
    ).reshape(64, 4)
    high = lax.reduce_precision(vector, 8, 7)
    vector = jnp.concatenate([high, vector - high], axis=1)
    vector = jnp.pad(jnp.tile(vector, (GRAD_ROWS // 64, 1)), ((0, 0), (90, 30)))
    (early_grad,) = kernel_call(
        early_grad_kernel,
        D // GRAD_ROWS,
        ids,
        [
            (normed, lanes(SPAN, GRAD_ROWS)),
            (early_part, whole(SPAN, 768)),
            (mix, whole(SPAN, 256)),
            (feed_gain_part, lanes(8, GRAD_ROWS)),
            (vector, whole(GRAD_ROWS, 128)),
        ]
        + [(part, lanes(*part.shape[:-1], GRAD_ROWS)) for part in span_mixed],
        [(shape(D, 1024, kind=bf16), blocks(GRAD_ROWS, 1024))],
        [pltpu.VMEM((SPAN, GRAD_ROWS), bf16)],
        flops=2 * SPAN * D * 1024,
    )
    dq, early_grad = lax.optimization_barrier((dq, early_grad))
    early_grad = jnp.sum(
        exchange(early_grad.reshape(SPANS, -1, 1024), SEQ).astype(f32), axis=0
    )
    dkv_same, gq = kernel_call(
        attend_back_same_kernel,
        CHIPS,
        ids,
        [(q, whole(SPAN, 128)), (same, kv_spec)] + back_ins
        + [(dq, whole(128, SPAN)), (dkv_other, blocks(1, SPAN, 128))],
        [dkv_shape, (shape(SPAN, 128, kind=bf16), whole(SPAN, 128))],
        [pltpu.VMEM((128, SPAN), f32)],
        flops=2 * 5 * SPAN * SPAN * 256 * 5,
    )
    dkv_same, early_grad, feed_grad, feed_parts = lax.optimization_barrier(
        (dkv_same, early_grad, feed_grad, feed_parts)
    )
    dkv_own = exchange(dkv_same, "chip")
    *normed_parts, mixer_gain_part = kernel_call(
        normed_back_kernel,
        SPAN // CHUNK,
        ids,
        [
            (early_part, blocks(CHUNK, 768)),
            (gq, blocks(CHUNK, 128)),
            (early, whole(D, 768)),
            (normed, blocks(CHUNK, D)),
            (gains, whole(8, D)),
        ],
        [pair_out] * 4 + [(shape(8, D), whole(8, D))],
        [pltpu.VMEM((CHUNK, 768), bf16)],
        flops=2 * SPAN * D * 768,
    )
    feed_own, feed_beside = sum_along_x(feed_parts, ids)
    feed_beside = beside_y(feed_beside)
    layer_output = (residual + feed_own + feed_beside.astype(f32)).astype(bf16)
    dkv_own = jnp.sum(dkv_own.astype(f32), axis=0).astype(bf16)
    normed_parts = along_x(normed_parts)
    gkv = exchange(dkv_own.reshape(8, own, 128), "head")
    (attend_grads,) = kernel_call(
        attend_grad_kernel,
        D // GRAD_ROWS,
        ids,
        [
            (normed, lanes(SPAN, GRAD_ROWS)),
            (gq, whole(SPAN, 128)),
            (dkv_own, whole(SPAN, 128)),
            (early, pl.BlockSpec((GRAD_ROWS, 256), lambda i, ids: (i, 3))),
            (gains, lanes(8, GRAD_ROWS)),
            (mixer_gain_part, lanes(8, GRAD_ROWS)),
        ],
        [(shape(D, 384, kind=bf16), blocks(GRAD_ROWS, 384))],
        flops=2 * SPAN * D * 640,
    )
    gkv, attend_grads, normed_parts = lax.optimization_barrier((gkv, attend_grads, normed_parts))
    attend_grads = exchange(attend_grads.reshape(SPANS, -1, 384), SEQ)
    normed_own, normed_beside = sum_along_x(normed_parts, ids)
    normed_beside = beside_y(normed_beside)
    (input_grad,) = kernel_call(
        input_kernel,
        1,
        ids,
        [
            (gkv, whole(8, own, 128)),
            (early, pl.BlockSpec((D, 256), lambda i, ids: (0, 3))),
            (normed_own, whole(own, D)),
            (normed_beside, whole(own, D)),
            (layer_input, whole(own, D)),
            (gains, whole(8, D)),
            (grad_residual, whole(own, D)),
        ],
        [(shape(own, D), whole(own, D))],
        flops=2 * own * D * 256,
    )
    attend_grads = jnp.sum(attend_grads.astype(f32), axis=0)
    common_grad = jnp.concatenate(
        [early_grad[:, 448:472], attend_grads[:, :1], early_grad[:, 473:768], attend_grads[:, 128:]],
        axis=1,
    )
    common_grad = jnp.sum(
        exchange(common_grad.astype(bf16).reshape(8, 8, 576), "head").astype(f32), axis=0
    )
    vector = (early_grad[:, 474:478] + early_grad[:, 478:482]).reshape(256)
    return (
        layer_output,
        input_grad,
        jnp.concatenate([common_grad[:, 64:], common_grad[:, :24]], axis=1),
        common_grad[:, 24],
        common_grad[:, 25],
        jnp.stack([early_grad[:, :192], early_grad[:, 256:448]], axis=1),
        attend_grads[:, 64:128],
        early_grad[:, 768:960],
        early_grad[:, 960:],
        feed_grad[:, :512].reshape(-1, 2, 256),
        feed_grad[:, 512:],
        vector[192:195],
        vector[195:198],
        vector[:192],
    )


def solution(mesh):
    devices = mesh.devices.reshape(CHIPS, 2, mesh.shape["head"])
    every = (*SEQ, "head")
    return jax.shard_map(
        shards,
        mesh=jax.sharding.Mesh(devices, every),
        in_specs=(
            P(every, None),
            P(every, None),
            P(every),
            P(every),
            P(SEQ, None, "head"),
            P(SEQ, "head"),
            P(SEQ, "head"),
            P(SEQ, "head"),
            P(SEQ, None, "head"),
            P(SEQ, "head"),
            P("head"),
            P("head"),
            P("head"),
            P(every, None),
        ),
        out_specs=(
            P(every, None),
            P(every, None),
            P(every, None),
            P(every),
            P(every),
            P(SEQ, None, "head"),
            P(SEQ, "head"),
            P(SEQ, "head"),
            P(SEQ, "head"),
            P(SEQ, None, "head"),
            P(SEQ, "head"),
            P("head"),
            P("head"),
            P("head"),
        ),
        check_vma=False,
    )
```

```python
import jax
import jax.numpy as jnp
from jax import lax
from jax.experimental import pallas as pl
from jax.experimental.pallas import tpu as pltpu
from jax.sharding import PartitionSpec as P

HEAD_DIM = 64
STATE = 128
ATT_HEADS = 8
KV_HEADS = 2
HEADS = 3
SPAN = 1024
GRAD_ROWS = 512
FEED_ROWS = 512
KEYS = 512
BACK_KEYS = 256
PER = 2
ROWS = 512
CHUNK = 256
SPANS = 16
CHIPS = 8
SEQ = ("chip", "core")
WIDE = 256
PACK = 1280

norm_eps = 1e-05
masked_score = -1e30
f32, bf16 = jnp.float32, jnp.bfloat16
MIB = 1024 * 1024


def gather(part, axis):
    size = lax.axis_size(axis)
    return lax.all_to_all(jnp.broadcast_to(part[None], (size,) + part.shape), axis, 0, 0)


def beside_y(part):
    return lax.ppermute(part, "head", [(k, k ^ 1) for k in range(8)])


def along_x(pairs):
    return [pairs[0]] + [
        lax.ppermute(pairs[d], "head", [(k, (k + 2 * d) % 8) for k in range(8)])
        for d in (1, 2, 3)
    ]


def shift_x(part, distance):
    return lax.ppermute(part, "head", [(k, (k + 2 * distance) % 8) for k in range(8)])


def near_x(own, beside):
    return [shift_x(own, 1), shift_x(beside, 1), shift_x(own, 3), shift_x(beside, 3)]


def relayed(own, beside, near):
    far = [shift_x(near[0], 1), shift_x(near[3], 3)]
    return [own, beside, *near[:2], *far, *near[2:]]


def other_core(part):
    return lax.ppermute(part, "core", [(0, 1), (1, 0)])


def exchange(pieces, axis):
    return lax.all_to_all(pieces, axis, 0, 0)


def rows(stacked):
    return stacked.reshape((-1,) + stacked.shape[2:])


def whole(*shape):
    return pl.BlockSpec(shape, lambda i, ids: (0,) * len(shape))


def blocks(*shape):
    return pl.BlockSpec(shape, lambda i, ids: (i,) + (0,) * (len(shape) - 1))


def lanes(*shape):
    return pl.BlockSpec(shape, lambda i, ids: (0,) * (len(shape) - 1) + (i,))


def backwards(spec, steps):
    index = spec.index_map
    return pl.BlockSpec(spec.block_shape, lambda i, ids: index(steps - 1 - i, ids))


def kernel_call(body, grid, ids, ins, outs, scratch=(), flops=0, limit=60):
    arrays, in_specs = zip(*ins)
    shapes, out_specs = zip(*outs)
    moved = sum(a.size * a.dtype.itemsize for a in arrays) + sum(
        s.size * s.dtype.itemsize for s in shapes
    )
    return pl.pallas_call(
        body,
        grid_spec=pltpu.PrefetchScalarGridSpec(
            num_scalar_prefetch=1,
            grid=(grid,),
            in_specs=list(in_specs),
            out_specs=list(out_specs),
            scratch_shapes=list(scratch),
        ),
        out_shape=list(shapes),
        compiler_params=pltpu.CompilerParams(
            dimension_semantics=("arbitrary",), vmem_limit_bytes=limit * MIB
        ),
        cost_estimate=pl.CostEstimate(flops=flops, bytes_accessed=moved, transcendentals=0),
    )(ids, *arrays)


def shape(*dims, kind=f32):
    return jax.ShapeDtypeStruct(dims, kind)


def dot(a, b):
    return jnp.dot(a, b, preferred_element_type=f32)


def dot_nt(a, b):
    return lax.dot_general(a, b, (((1,), (1,)), ((), ())), preferred_element_type=f32)


def dot_tn(a, b):
    return lax.dot_general(a, b, (((0,), (0,)), ((), ())), preferred_element_type=f32)


def select_sum(a, b):
    high = a.astype(bf16)
    return dot(high, b) + dot((a - high.astype(f32)).astype(bf16), b)


def iota(dims, axis):
    return lax.broadcasted_iota(jnp.int32, dims, axis)


def spread(columns, base):
    lane = iota((columns.shape[0], WIDE), 1)
    c = [columns[:, base + h : base + h + 1] for h in range(HEADS)]
    return jnp.where(
        lane < 64, c[0], jnp.where(lane < 128, c[1], jnp.where(lane < 192, c[2], 0.0))
    )


def spread_rows(parts):
    row = iota((WIDE, STATE), 0)
    return jnp.where(
        row < 64, parts[0], jnp.where(row < 128, parts[1], jnp.where(row < 192, parts[2], 0.0))
    )


def head_select(offset):
    lane, column = iota((WIDE, 128), 0), iota((WIDE, 128), 1)
    return jnp.where((column == offset + lane // 64) & (lane < 192), 1.0, 0.0).astype(bf16)


def head_mean(values):
    a, b = iota((WIDE, WIDE), 0), iota((WIDE, WIDE), 1)
    return select_sum(values, jnp.where(a // 64 == b // 64, 1.0 / 64, 0.0).astype(bf16))


def prefix_sum(values):
    width = values.shape[1]
    lane = iota(values.shape, 1)
    step = 1
    while step < width:
        values = values + jnp.where(lane >= step, pltpu.roll(values, step, 1), 0.0)
        step *= 2
    return values


def suffix_sum(values):
    width = values.shape[1]
    lane = iota(values.shape, 1)
    step = 1
    while step < width:
        values = values + jnp.where(lane < width - step, pltpu.roll(values, width - step, 1), 0.0)
        step *= 2
    return values


def columns_of(parts):
    n = parts[0].shape[1]
    full = jnp.concatenate(list(parts) + [jnp.zeros((128 - 8 * len(parts), n), f32)], axis=0)
    return full.T


def by_distance(refs):
    if len(refs) == 8:
        return list(zip(refs[0::2], refs[1::2]))
    return [(ref.at[0], ref.at[1]) for ref in refs]


def span_rows(ids, first, refs, tokens):
    head = ids[1]
    beside = lax.rem(head, 2)
    for n in range(tokens.shape[0] // 256):
        distance = lax.rem(head // 2 - (first + n) + 4, 4)
        mine = pl.multiple_of(256 * n + 128 * beside, 128)
        theirs = pl.multiple_of(256 * n + 128 - 128 * beside, 128)
        for d, pair in enumerate(by_distance(refs)):

            @pl.when(distance == d)
            def _(pair=pair, mine=mine, theirs=theirs):
                tokens[pl.ds(mine, 128), :] = pair[0][...]
                tokens[pl.ds(theirs, 128), :] = pair[1][...]


def project_kernel(ids, *refs):
    inputs, (same, other, params) = refs[:8], refs[8:11]
    normed, x_out, gate_out, wr_out, q_out, col_out, row_out = refs[11:18]
    states, pack, gains, weights, carry, total, tokens = refs[18:]
    i = pl.program_id(0)
    head = ids[1]
    kv_head = head // (ATT_HEADS // KV_HEADS)

    @pl.when(i == 0)
    def _():
        carry[...] = jnp.zeros_like(carry)
        total[...] = jnp.zeros_like(total)
        for c in range(CHIPS):
            for part, core in ((same, ids[3]), (other, 1 - ids[3])):
                first = pl.multiple_of((2 * c + core) * 64, 64)
                weights[pl.ds(first, 64), :] = part[c, :, :1024]
        gains[...] = weights[:, 384:512].astype(f32).T[88:96]
        for c in range(CHIPS):
            pack[c, SPAN:, :] = jnp.zeros((PACK - SPAN, 128), bf16)

    span_rows(ids, PER * i, inputs, tokens)
    values = tokens[...].astype(f32)
    scale = lax.rsqrt(jnp.mean(values * values, axis=1, keepdims=True) + norm_eps)
    low = (values * scale * gains[0:1, :]).astype(bf16)
    normed[...] = low
    made = dot(low, weights[...])
    wide_lane = iota((ROWS, WIDE), 1)
    lane = iota((ROWS, 128), 1)
    x = jnp.where(wide_lane < 192, made[:, :256], 0.0).astype(bf16)
    x_out[...] = x
    gate_out[...] = jnp.where(wide_lane < 192, made[:, 256:512], 0.0)
    q = pltpu.roll(made[:, 128:256], 64, 1)
    q_out[...] = jnp.where(lane < 64, q.astype(bf16).astype(f32) * HEAD_DIM**-0.5, 0.0).astype(bf16)
    write = made[:, 512:640].astype(bf16)
    wr_out[:, :128] = write
    wr_out[:, 128:] = made[:, 640:768].astype(bf16)
    keys, vals = made[:, 768:896], made[:, 896:1024]
    first = kv_head == 0
    keys = jnp.where(first, keys, pltpu.roll(keys, 64, 1))
    vals = jnp.where(first, pltpu.roll(vals, 64, 1), vals)
    kv = jnp.where(lane < 64, keys, vals).astype(bf16)
    for c in range(CHIPS):
        pack[c, pl.ds(pl.multiple_of(i * ROWS, ROWS), ROWS), :] = kv

    misc = made[:, 384:512].astype(bf16).astype(f32)
    raws = pltpu.roll(misc, 64 - HEADS * head, 1).T[:8]
    own = iota((8, ROWS), 0) < HEADS
    z = jnp.where(own, raws, 0.0) + params[:, 0:1]
    step = jnp.where(own, jnp.log1p(jnp.exp(-jnp.abs(z))) + jnp.maximum(z, 0.0), 0.0)
    log_decay = -jnp.exp(params[:, 1:2]) * step
    row_out[8:16, :] = step
    row_out[16:24, :] = lax.logistic(z)
    parts = []
    for c in range(PER):
        here = slice(c * CHUNK, c * CHUNK + CHUNK)
        cum = prefix_sum(log_decay[:, here])
        row_out[0:8, here] = cum
        columns = columns_of([cum, step[:, here]])
        col_out[here, :] = columns
        last = cum[:, CHUNK - 1 : CHUNK]
        tail = jnp.exp(spread_last(last) - spread(columns, 0)) * spread(columns, 8)
        fresh = dot_tn((x[here].astype(f32) * tail).astype(bf16), write[here])
        parts.append((last, fresh))
    state, passed = carry[...], total[...]
    for c, (last, fresh) in enumerate(parts):
        states[c] = state
        grown = jnp.exp(last)
        state = spread_rows([grown[h : h + 1] for h in range(HEADS)]) * state + fresh
        passed = passed + jnp.broadcast_to(last, (8, 128))
    carry[...] = state
    total[...] = passed

    @pl.when(i == pl.num_programs(0) - 1)
    def _():
        state = carry[:192].astype(bf16)
        high = total[...].astype(bf16).astype(f32)
        decays = jnp.concatenate([high, total[...] - high], axis=0).astype(bf16)
        for c in range(CHIPS):
            pack[c, SPAN : SPAN + 192, :] = state
            pack[c, SPAN + 192 : SPAN + 208, :] = decays


def spread_last(last):
    lane = iota((1, WIDE), 1)
    return jnp.where(
        lane < 64,
        last[0:1],
        jnp.where(lane < 128, last[1:2], jnp.where(lane < 192, last[2:3], 0.0)),
    )


def combine_states(span_of, place, later):
    passed = jnp.zeros((8, 128), f32)
    entry = jnp.zeros((192, 128), f32)
    row = iota((192, 128), 0)
    order = range(SPANS) if later else reversed(range(SPANS))
    for k in order:
        use = (k > place) if later else (k < place)
        weight = jnp.where(use, jnp.exp(passed), 0.0)
        weights = jnp.where(
            row < 64, weight[0:1], jnp.where(row < 128, weight[1:2], weight[2:3])
        )
        span = span_of(k).astype(f32)
        entry = entry + weights * span[0:192]
        decay = span[192:200] + span[200:208]
        passed = passed + jnp.where(use, decay, 0.0)
    return jnp.concatenate([entry, jnp.zeros((64, 128), f32)], axis=0)


def scan_kernel(
    ids, x_ref, gate_ref, wr_ref, col_ref, row_ref, local, same, other, gain,
    y_out, low_out, state_out,
    carried,
):
    i = pl.program_id(0)

    @pl.when(i == 0)
    def _():
        carried[...] = combine_states(
            lambda k: jnp.where(ids[3] == k % 2, same[k // 2, :208], other[k // 2, :208]),
            ids[0],
            False,
        )

    passed = carried[...]
    entries = []
    for c in range(PER):
        entries.append(local[c] + passed)
        grown = jnp.exp(row_ref[0:8, c * CHUNK + CHUNK - 1 : c * CHUNK + CHUNK])
        passed = spread_rows([grown[h : h + 1] for h in range(HEADS)]) * passed
    carried[...] = passed
    causal = iota((CHUNK, CHUNK), 0) >= iota((CHUNK, CHUNK), 1)
    wide_lane = iota((CHUNK, WIDE), 1)
    for c, entry in enumerate(entries):
        here = slice(c * CHUNK, c * CHUNK + CHUNK)
        state_out[c] = entry
        columns = col_ref[here, :]
        write, read = wr_ref[here, :128], wr_ref[here, 128:]
        cum = spread(columns, 0)
        scaled = (x_ref[here, :].astype(f32) * spread(columns, 8)).astype(bf16)
        products = dot_nt(read, write)
        y = jnp.exp(cum) * dot_nt(read, entry.astype(bf16))
        for h in range(HEADS):
            span = columns[:, h : h + 1] - row_ref[h : h + 1, here]
            weights = jnp.exp(jnp.where(causal, span, masked_score)) * products
            part = jnp.where(wide_lane // 64 == h, scaled, jnp.zeros_like(scaled))
            y = y + dot(weights.astype(bf16), part)
        y_out[here, :] = y
        gate = gate_ref[here, :]
        gated = y * (gate * lax.logistic(gate))
        low = gated * lax.rsqrt(head_mean(gated * gated) + norm_eps) * gain[...]
        low_out[here, :] = low.astype(bf16)


def attend_visit(kv_ref, q_ref, peak, accum, masked):
    before = now = peak[0:1, :]
    blocks_of = []
    for first in range(0, SPAN, KEYS):
        kv = kv_ref[0, first : first + KEYS, :]
        scores = dot_nt(kv, q_ref[...])
        if masked:
            dims = (KEYS, SPAN)
            scores = jnp.where(iota(dims, 0) + first > iota(dims, 1), masked_score, scores)
        now = jnp.maximum(now, jnp.max(scores, axis=0, keepdims=True))
        blocks_of.append((kv, scores))
    total = accum[...] * jnp.exp(before - now)
    for kv, scores in blocks_of:
        ones = jnp.where(iota(kv.shape, 1) < 64, jnp.ones_like(kv), kv)
        total = total + dot_tn(ones, jnp.exp(scores - now).astype(bf16))
    accum[...] = total
    peak[...] = jnp.broadcast_to(now, peak.shape)


def attend_own_kernel(ids, q_ref, kv_ref, peak, accum):
    peak[...] = jnp.full_like(peak, masked_score)
    accum[...] = jnp.zeros_like(accum)
    attend_visit(kv_ref, q_ref, peak, accum, True)


def attend_same_kernel(ids, q_ref, kv_ref, peak_in, accum_in, peak, accum):
    k = pl.program_id(0)

    @pl.when(k == 0)
    def _():
        peak[...] = peak_in[...]
        accum[...] = accum_in[...]

    @pl.when(k < ids[2])
    def _():
        attend_visit(kv_ref, q_ref, peak, accum, False)


def attend_other_kernel(
    ids, q_ref, kv_ref, low_ref, peak_in, accum_in, mix_out, o_out, lse_out, peak, accum
):
    k = pl.program_id(0)

    @pl.when(k == 0)
    def _():
        peak[...] = peak_in[...]
        accum[...] = accum_in[...]

    @pl.when(k < ids[2] + ids[3])
    def _():
        attend_visit(kv_ref, q_ref, peak, accum, False)

    @pl.when(k == pl.num_programs(0) - 1)
    def _():
        lane = iota((SPAN, 128), 1)
        total = accum[0:1, :]
        out = (accum[...] / total).T
        o_out[...] = out
        mix_out[:, :128] = low_ref[:, :128]
        mix_out[:, 128:] = jnp.where(lane < 64, low_ref[:, 128:], out.astype(bf16))
        lse_out[...] = peak[...] + jnp.log(total)


def by_head(ids, refs):
    head = ids[1]
    for d, pair in enumerate(by_distance(refs)):
        x = lax.rem(head // 2 - d + 4, 4)
        for t in range(2):
            yield 2 * x + lax.rem(head + t, 2), pair[t]


def residual_kernel(ids, mix, *refs):
    weight_refs, (inp, gains, residual_out, feed_out) = refs[:8], refs[8:]
    total = jnp.zeros(residual_out.shape, f32)
    for h, weights in by_head(ids, weight_refs):
        total = total + dot_nt(mix[h], weights[...])
    residual = inp[...].astype(f32) + total
    residual_out[...] = residual
    scale = lax.rsqrt(jnp.mean(residual * residual, axis=1, keepdims=True) + norm_eps)
    feed = (residual * scale * gains[1:2, :]).astype(bf16)
    for h in range(8):
        feed_out[h] = feed


def by_x(ids, first, part, outs):
    beside = lax.rem(ids[1], 2)
    for n in range(part.shape[0] // 256):
        distance = lax.rem(first + n - ids[1] // 2 + 4, 4)
        for d, out in enumerate(outs):

            @pl.when(distance == d)
            def _(out=out, n=n):
                out[beside] = part[256 * n : 256 * n + 128]
                out[1 - beside] = part[256 * n + 128 : 256 * n + 256]


def feed_kernel(ids, feed, *refs):
    weights, *parts, back_out, units_out, hidden_out, cot = refs[8:]
    first = pl.program_id(0) * (FEED_ROWS // 256)
    span_rows(ids, first, refs[:8], cot)
    hidden = dot(feed[...], weights[:, :512])
    gate, up = hidden[:, :256], hidden[:, 256:]
    sig = lax.logistic(gate)
    swish = gate * sig
    units = (swish * up).astype(bf16)
    units_out[...] = units
    down = weights[:, 512:768]
    part = dot_nt(units, down).astype(bf16)
    by_x(ids, first, part, parts)
    grad_units = dot(cot[...], down)
    grad_gate = grad_units * up * (sig * (1.0 + gate * (1.0 - sig)))
    grad_hidden = jnp.concatenate([grad_gate, grad_units * swish], axis=1).astype(bf16)
    hidden_out[...] = grad_hidden
    back_out[...] = dot_nt(grad_hidden, weights[:, :512]).astype(bf16)


def mixed_kernel(ids, back, residual_ref, cot, gains, *refs):
    weight_refs, (grad_out, copies, gain_out, parts) = refs[:8], refs[8:]
    grad_feed = back[0].astype(f32)
    for h in range(1, 8):
        grad_feed = grad_feed + back[h].astype(f32)
    residual = residual_ref[...]
    scale = lax.rsqrt(jnp.mean(residual * residual, axis=1, keepdims=True) + norm_eps)
    normal = residual * scale
    gain_out[...] = jnp.broadcast_to(
        jnp.sum(grad_feed * normal, axis=0, keepdims=True), gain_out.shape
    )
    w = grad_feed * gains[1:2, :]
    grad = cot[...].astype(f32) + scale * (
        w - normal * jnp.mean(w * normal, axis=1, keepdims=True)
    )
    grad_out[...] = grad
    low = grad.astype(bf16)
    copies[...] = low
    for h, weights in by_head(ids, weight_refs):
        parts[h] = dot(low, weights[...]).astype(bf16)


def gate_back_kernel(
    ids, grad_ref, y_ref, gate_ref, gain, wr_ref, col_ref, row_ref, o_ref, decays,
    gy_out, ggate_out, do_out, delta_out, pack, gain_out,
    carry,
):
    i = pl.program_id(0)

    @pl.when(i == 0)
    def _():
        carry[...] = jnp.zeros_like(carry)
        gain_out[...] = jnp.zeros_like(gain_out)

    wide_lane = iota((ROWS, WIDE), 1)
    lane = iota((ROWS, 128), 1)
    own = wide_lane < 192
    grad_all = grad_ref[...].astype(f32)
    grad = jnp.where(own, grad_all, 0.0)
    grad_out = jnp.where(lane < 64, 0.0, grad_all[:, 128:])
    do_out[...] = grad_out.astype(bf16)
    delta = jnp.sum((grad_out * o_ref[...]).T, axis=0, keepdims=True)
    delta_out[...] = jnp.broadcast_to(delta, (8, ROWS))
    y, gate = y_ref[...], gate_ref[...]
    sig = lax.logistic(gate)
    swish = gate * sig
    m = y * swish
    q = lax.rsqrt(head_mean(m * m) + norm_eps)
    gain_out[...] += jnp.broadcast_to(jnp.sum(grad * m * q, axis=0, keepdims=True), (8, WIDE))
    w = grad * gain[...]
    grad_gated = q * (w - m * (q * q) * head_mean(w * m))
    gy = grad_gated * swish
    gy_out[...] = gy
    ggate_out[...] = (grad_gated * y * (sig * (1.0 + gate * (1.0 - sig)))).astype(bf16)
    weighted = (gy * jnp.exp(spread(col_ref[...], 0))).astype(bf16)
    state = carry[...]
    for c in reversed(range(PER)):
        here = slice(c * CHUNK, c * CHUNK + CHUNK)
        grown = jnp.exp(row_ref[0:8, c * CHUNK + CHUNK - 1 : c * CHUNK + CHUNK])
        state = spread_rows([grown[h : h + 1] for h in range(HEADS)]) * state + dot_tn(
            weighted[here], wr_ref[here, 128:]
        )
    carry[...] = state

    @pl.when(i == pl.num_programs(0) - 1)
    def _():
        state = carry[:192].astype(bf16)
        for c in range(SPANS):
            pack[c, :192, :] = state
            pack[c, 192:208, :] = decays[0, 192:208, :]


def attend_back_visit(refs, masked, arrived=None):
    q_ref, kv_ref, do_ref, lse, delta, dkv_out, accum = refs
    for first in range(0, SPAN, BACK_KEYS):
        here = slice(first, first + BACK_KEYS)
        seen = slice(first if masked else 0, SPAN)
        kv, q, grad = kv_ref[0, here, :], q_ref[seen, :], do_ref[seen, :]
        scores = dot_nt(kv, q)
        if masked:
            scores = jnp.where(
                iota(scores.shape, 0) > iota(scores.shape, 1), masked_score, scores
            )
        probs = jnp.exp(scores - lse[0:1, seen])
        grad_scores = (probs * (dot_nt(kv, grad) - delta[0:1, seen])).astype(bf16)
        dkv = dot(probs.astype(bf16), grad) + dot(grad_scores, q)
        if arrived is not None:
            dkv = dkv + arrived[0, here, :].astype(f32)
        dkv_out[0, here, :] = dkv.astype(bf16)
        accum[:, seen] += dot_tn(kv, grad_scores)


def attend_back_other_kernel(ids, q_ref, kv_ref, do_ref, lse, delta, dkv_out, dq_out):
    k = pl.program_id(0)
    seen = ids[2] + ids[3]

    @pl.when(k == 0)
    def _():
        dq_out[...] = jnp.zeros_like(dq_out)

    @pl.when(k < seen)
    def _():
        attend_back_visit((q_ref, kv_ref, do_ref, lse, delta, dkv_out, dq_out), False)

    @pl.when(k >= seen)
    def _():
        dkv_out[...] = jnp.zeros_like(dkv_out)


def attend_back_same_kernel(
    ids, q_ref, kv_ref, do_ref, lse, delta, dq_in, arrived, dkv_out, dq_out, accum
):
    k = pl.program_id(0)
    refs = (q_ref, kv_ref, do_ref, lse, delta, dkv_out, accum)

    @pl.when(k == 0)
    def _():
        accum[...] = dq_in[...]

    @pl.when(k < ids[2])
    def _():
        attend_back_visit(refs, False, arrived)

    @pl.when(k == ids[2])
    def _():
        attend_back_visit(refs, True, arrived)
        dq = pltpu.roll((accum[...] * HEAD_DIM**-0.5).T, 64, 1)
        dq_out[...] = jnp.where(iota((SPAN, 128), 1) < 64, 0.0, dq).astype(bf16)

    @pl.when(k > ids[2])
    def _():
        dkv_out[...] = arrived[...]


def feed_grad_kernel(ids, feed, units, hidden, *refs):
    out, cot = refs[8:]
    span_rows(ids, 0, refs[:8], cot)
    out[:, :512] = dot_tn(feed[...], hidden[...]).astype(bf16)
    out[:, 512:] = dot_tn(cot[...], units[...]).astype(bf16)


def early_grad_kernel(ids, normed, grad, mix, feed_part, vector, *refs):
    out, mixed = refs[4:]
    span_rows(ids, 0, refs[:4], mixed)
    made = dot_tn(normed[...], grad[...])
    both = jnp.where(iota((8, GRAD_ROWS), 0) == 0, feed_part[...], 0.0)
    columns = pltpu.roll(columns_of([both]), 89, 1) + vector[...]
    out[:, :384] = made[:, :384].astype(bf16)
    out[:, 384:512] = (made[:, 384:512] + columns).astype(bf16)
    out[:, 512:768] = made[:, 512:].astype(bf16)
    out[:, 768:] = dot_tn(mixed[...], mix[...]).astype(bf16)


def attend_grad_kernel(ids, normed_ref, gq, gkv_ref, weights, gains, gain_ref, out):
    normed = normed_ref[...]
    lane = iota((SPAN, 128), 1)
    gkv = gkv_ref[...].astype(f32)
    turned = pltpu.roll(gkv, 64, 1)
    first = ids[1] // (ATT_HEADS // KV_HEADS) == 0
    low_lanes = lane < 64
    place = jnp.where(first, low_lanes.astype(jnp.int32), 1 - low_lanes.astype(jnp.int32)) == 1
    keys = jnp.where(place, jnp.where(first, gkv, turned), 0.0)
    vals = jnp.where(place, jnp.where(first, turned, gkv), 0.0)
    both = jnp.concatenate([keys, vals], axis=1).astype(bf16)
    made = dot_tn(normed, jnp.concatenate([gq[...], both], axis=1))
    normal = normed.astype(f32) / gains[0:1, :]
    gain = jnp.sum(dot_nt(both, weights[...]) * normal, axis=0, keepdims=True) + gain_ref[0:1, :]
    gain = jnp.where(iota((8, GRAD_ROWS), 0) == 0, gain, 0.0)
    out[:, :128] = (made[:, :128] + columns_of([gain])).astype(bf16)
    out[:, 128:] = made[:, 128:].astype(bf16)


def scan_back_kernel(
    ids, x_ref, gy_ref, wr_ref, col_ref, row_ref, state_ref, adjoints, params, ggate_ref,
    grad_out, sums,
    carry,
):
    i = pl.program_id(0)

    @pl.when(i == 0)
    def _():
        carry[...] = combine_states(lambda k: adjoints[k], ids[0], True)
        sums[...] = jnp.zeros_like(sums)

    refs = (x_ref, gy_ref, wr_ref, col_ref, row_ref, state_ref, params, ggate_ref)
    later = carry[...]
    for c in reversed(range(PER)):
        later = scan_back_chunk(ids, c, later, refs, grad_out, sums)
    carry[...] = later


def scan_back_chunk(ids, c, later, refs, grad_out, sums):
    x_ref, gy_ref, wr_ref, col_ref, row_ref, state_ref, params, ggate_ref = refs
    here = slice(c * CHUNK, c * CHUNK + CHUNK)
    columns = col_ref[here, :]
    write, read = wr_ref[here, :128], wr_ref[here, 128:]
    entry = state_ref[c]
    later_low, entry_low = later.astype(bf16), entry.astype(bf16)
    x, gy = x_ref[here, :].astype(f32), gy_ref[here, :]
    gy_low = gy.astype(bf16)
    step = spread(columns, 8)
    cum = spread(columns, 0)
    last = row_ref[0:8, c * CHUNK + CHUNK - 1 : c * CHUNK + CHUNK]
    scaled = x * step
    scaled_low = scaled.astype(bf16)
    left = jnp.exp(spread_last(last) - cum)
    entered = jnp.exp(cum)
    products = dot_nt(write, read)
    causal = iota((CHUNK, CHUNK), 0) <= iota((CHUNK, CHUNK), 1)
    wide_lane = iota((CHUNK, WIDE), 1)
    lane = iota((CHUNK, 128), 1)
    from_later = left * dot_nt(write, later_low)
    u = from_later
    summed = jnp.zeros((CHUNK, CHUNK), f32)
    row_sums = jnp.zeros((8, CHUNK), f32)
    col_sums = jnp.zeros((CHUNK, 128), f32)
    head_row = iota((8, CHUNK), 0)
    for h in range(HEADS):
        mine = wide_lane // 64 == h
        span = row_ref[h : h + 1, here] - columns[:, h : h + 1]
        decay = jnp.exp(jnp.where(causal, span, masked_score))
        gy_part = jnp.where(mine, gy_low, jnp.zeros_like(gy_low))
        u = u + dot((decay * products).astype(bf16), gy_part)
        terms = decay * dot_nt(scaled_low, gy_part)
        summed = summed + terms
        terms = terms * products
        row_sums = row_sums + jnp.where(
            head_row == h, jnp.sum(terms, axis=0, keepdims=True), 0.0
        )
        col_sums = col_sums + jnp.where(lane == h, jnp.sum(terms, axis=1, keepdims=True), 0.0)
    grad_out[here, :256] = (step * u).astype(bf16)
    low = summed.astype(bf16)
    grad_out[here, 512:640] = (dot(low, read) + dot((scaled * left).astype(bf16), later_low)).astype(bf16)
    entered_gy = (gy * entered).astype(bf16)
    grad_out[here, 640:768] = (dot_tn(low, write) + dot(entered_gy, entry_low)).astype(bf16)
    carried_part = gy * (entered * dot_nt(read, entry_low))
    listed = (
        select_sum(carried_part, head_select(0))
        - col_sums
        + select_sum(scaled * from_later, head_select(8))
        + select_sum(x * u, head_select(16))
    ).T
    meet = later * entry
    grown = jnp.exp(last)
    eight = iota((8, 1), 0)
    constant = jnp.zeros((8, 1), f32)
    for h in range(HEADS):
        part = jnp.sum(meet[64 * h : 64 * h + 64], axis=0, keepdims=True)
        constant = constant + jnp.where(eight == h, jnp.sum(part, axis=1, keepdims=True), 0.0)
    tails = listed[8:16]
    grad_log = (
        suffix_sum(row_sums + listed[0:8]) + (prefix_sum(tails) - tails) + grown * constant
    )
    rate = jnp.exp(params[:, 1:2])
    grad_raw = (listed[16:24] - rate * grad_log) * row_ref[16:24, here]
    grad_raw = jnp.where(head_row < HEADS, grad_raw, 0.0)
    log_decay = -rate * row_ref[8:16, here]
    rate_sum = jnp.sum(grad_log * log_decay, axis=1, keepdims=True)
    bias_sum = jnp.sum(grad_raw, axis=1, keepdims=True)
    sums[...] += jnp.where(iota((8, 128), 1) == 0, rate_sum, bias_sum)
    steps = pltpu.roll(columns_of([grad_raw]), 64 + HEADS * ids[1], 1).astype(bf16)
    grad_out[here, 256:384] = ggate_ref[here, :128]
    grad_out[here, 384:512] = jnp.where(lane < 64, ggate_ref[here, 128:], steps)
    return spread_rows([grown[h : h + 1] for h in range(HEADS)]) * later + dot_tn(
        entered_gy, read
    )


def normed_back_kernel(
    ids, early, gq, weights, normed, gains, out_0, out_1, out_2, out_3, gain_out, grad
):
    i = pl.program_id(0)

    @pl.when(i == 0)
    def _():
        gain_out[...] = jnp.zeros_like(gain_out)

    grad[...] = early[...]
    grad[:, 128:256] = jnp.where(iota((CHUNK, 128), 1) < 64, early[:, 128:256], gq[...])
    part = dot_nt(grad[...], weights[...])
    normal = normed[...].astype(f32) / gains[0:1, :]
    gain_out[...] += jnp.broadcast_to(
        jnp.sum(part * normal, axis=0, keepdims=True), gain_out.shape
    )
    by_x(ids, i, part.astype(bf16), (out_0, out_1, out_2, out_3))


def along_x_kernel(ids, part_0, part_1, part_2, part_3, own, beside):
    parts = (part_0, part_1, part_2, part_3)
    own[...] = sum(part[0].astype(f32) for part in parts)
    beside[...] = sum(part[1].astype(f32) for part in parts).astype(bf16)


def input_kernel(
    ids, gkv_ref, weights, own, beside, inp, gains, residual_grad, out
):
    lane = iota((128, 128), 1)
    group = ATT_HEADS // KV_HEADS
    gkv = [
        sum(gkv_ref[h].astype(f32) for h in range(group * n, group * n + group))
        for n in range(KV_HEADS)
    ]
    keys = jnp.where(lane < 64, gkv[0], pltpu.roll(gkv[1], 64, 1))
    vals = jnp.where(lane < 64, pltpu.roll(gkv[0], 64, 1), gkv[1])
    both = jnp.concatenate([keys, vals], axis=1).astype(bf16)
    grad = own[...] + beside[...].astype(f32) + dot_nt(both, weights[...])
    values = inp[...].astype(f32)
    scale = lax.rsqrt(jnp.mean(values * values, axis=1, keepdims=True) + norm_eps)
    normal = values * scale
    w = grad * gains[0:1, :]
    out[...] = residual_grad[...] + scale * (
        w - normal * jnp.mean(w * normal, axis=1, keepdims=True)
    )


def sum_along_x(parts, ids):
    own, D = parts[0].shape[1:]
    return kernel_call(
        along_x_kernel,
        1,
        ids,
        [(part, whole(2, own, D)) for part in parts],
        [(shape(own, D), whole(own, D)), (shape(own, D, kind=bf16), whole(own, D))],
    )


def shards(
    layer_input,
    shared_weight,
    mixer_gain,
    feed_gain,
    branch_weight,
    query_weight,
    mamba_weight,
    attend_weight,
    hidden_weight,
    down_weight,
    rate_log,
    step_bias,
    mamba_gain,
    cotangent,
):
    chip, core, head_index = (lax.axis_index(name) for name in ("chip", "core", "head"))
    ids = jnp.stack([2 * chip + core, head_index, chip, core]).astype(jnp.int32)
    steps = SPAN // ROWS
    D = layer_input.shape[1]
    own = layer_input.shape[0]

    common = jnp.concatenate(
        [
            shared_weight[:, 512:],
            mixer_gain[:, None],
            feed_gain[:, None],
            jnp.zeros((8, 38), bf16),
            shared_weight[:, :512],
        ],
        axis=1,
    )
    common = rows(gather(common, "head"))
    early = jnp.concatenate(
        [
            branch_weight[:, 0],
            query_weight,
            branch_weight[:, 1],
            common,
            mamba_weight,
            attend_weight,
        ],
        axis=1,
    )
    input_beside = beside_y(layer_input)
    input_near, early = lax.optimization_barrier((near_x(layer_input, input_beside), early))
    early_same = gather(early, "chip")
    early_same, span_input, cot_beside = lax.optimization_barrier(
        (early_same, relayed(layer_input, input_beside, input_near), beside_y(cotangent))
    )
    early_other = other_core(early_same)
    pair = jnp.stack([early_same[..., 1024:], early_other[..., 1024:]], axis=1)
    pair = jnp.where(core == 0, pair, pair[:, ::-1])
    mix_weights = pair.reshape(D, 256)
    mix_beside = beside_y(mix_weights)
    span_input = [(part, whole(*part.shape)) for part in span_input]
    params = jnp.pad(jnp.stack([step_bias, rate_log], axis=1), ((0, 5), (0, 126)))
    gain_row = jnp.pad(mamba_gain[None], ((0, 0), (0, 64)))
    early_spec = whole(CHIPS, 64, 1280)
    normed, x, gate, wr, q, col, row, local, pack, gains, early = kernel_call(
        project_kernel,
        steps,
        ids,
        span_input
        + [(early_same, early_spec), (early_other, early_spec), (params, whole(8, 128))],
        [
            (shape(SPAN, D, kind=bf16), blocks(ROWS, D)),
            (shape(SPAN, WIDE, kind=bf16), blocks(ROWS, WIDE)),
            (shape(SPAN, WIDE), blocks(ROWS, WIDE)),
            (shape(SPAN, 256, kind=bf16), blocks(ROWS, 256)),
            (shape(SPAN, 128, kind=bf16), blocks(ROWS, 128)),
            (shape(SPAN, 128), blocks(ROWS, 128)),
            (shape(24, SPAN), lanes(24, ROWS)),
            (shape(steps * PER, WIDE, STATE), blocks(PER, WIDE, STATE)),
            (shape(CHIPS, PACK, 128, kind=bf16), whole(CHIPS, PACK, 128)),
            (shape(8, D), whole(8, D)),
            (shape(D, 1024, kind=bf16), whole(D, 1024)),
        ],
        [
            pltpu.VMEM((WIDE, STATE), f32),
            pltpu.VMEM((8, 128), f32),
            pltpu.VMEM((ROWS, D), bf16),
        ],
        flops=2 * SPAN * D * 1024,
    )
    pack, mix_beside, cotangent_sent = lax.optimization_barrier((pack, mix_beside, cotangent))
    cot_near = near_x(cotangent_sent, cot_beside)
    same = exchange(pack, "chip")
    kv_spec = pl.BlockSpec((1, SPAN, 128), lambda i, ids: (jnp.minimum(i, ids[2]), 0, 0))
    peak_state = shape(8, SPAN), whole(8, SPAN)
    accum_state = shape(128, SPAN), whole(128, SPAN)
    peak, accum = kernel_call(
        attend_own_kernel,
        1,
        ids,
        [(q, whole(SPAN, 128)), (pack, whole(1, SPAN, 128))],
        [peak_state, accum_state],
        flops=2 * 2 * SPAN * SPAN * 256,
    )
    same, span_cot, peak, accum = lax.optimization_barrier(
        (same, relayed(cotangent, cot_beside, cot_near), peak, accum)
    )
    mix_near = near_x(mix_weights, mix_beside)
    late = jnp.concatenate([hidden_weight.reshape(-1, 512), down_weight], axis=1)
    late, same = lax.optimization_barrier((late, same))
    late = lax.all_gather(late, SEQ, axis=0, tiled=True)
    other = other_core(same)

    peak, accum = kernel_call(
        attend_same_kernel,
        CHIPS,
        ids,
        [
            (q, whole(SPAN, 128)),
            (same, kv_spec),
            (peak, whole(8, SPAN)),
            (accum, whole(128, SPAN)),
        ],
        [peak_state, accum_state],
        flops=2 * 2 * SPAN * SPAN * 256 * 5,
    )
    state_spec = pl.BlockSpec((CHIPS, 256, 128), lambda i, ids: (0, 4, 0))
    y, low, entries = kernel_call(
        scan_kernel,
        steps,
        ids,
        [
            (x, blocks(ROWS, WIDE)),
            (gate, blocks(ROWS, WIDE)),
            (wr, blocks(ROWS, 256)),
            (col, blocks(ROWS, 128)),
            (row, lanes(24, ROWS)),
            (local, blocks(PER, WIDE, STATE)),
            (same, state_spec),
            (other, state_spec),
            (gain_row, whole(1, WIDE)),
        ],
        [
            (shape(SPAN, WIDE), blocks(ROWS, WIDE)),
            (shape(SPAN, WIDE, kind=bf16), blocks(ROWS, WIDE)),
            (shape(steps * PER, WIDE, STATE), blocks(PER, WIDE, STATE)),
        ],
        [pltpu.VMEM((WIDE, STATE), f32)],
        flops=2 * SPAN * 256 * 256 * 8,
    )
    peak, low, mix_near = lax.optimization_barrier((peak, low, mix_near))
    mix_weights = relayed(mix_weights, mix_beside, mix_near)
    mix, o_pad, lse = kernel_call(
        attend_other_kernel,
        CHIPS,
        ids,
        [
            (q, whole(SPAN, 128)),
            (other, kv_spec),
            (low, whole(SPAN, WIDE)),
            (peak, whole(8, SPAN)),
            (accum, whole(128, SPAN)),
        ],
        [
            (shape(SPAN, 256, kind=bf16), whole(SPAN, 256)),
            (shape(SPAN, 128), whole(SPAN, 128)),
            (shape(8, SPAN), whole(8, SPAN)),
        ],
        [pltpu.VMEM((8, SPAN), f32), pltpu.VMEM((128, SPAN), f32)],
        flops=2 * 2 * SPAN * SPAN * 256 * 5,
    )
    mix, mix_weights = lax.optimization_barrier((mix, mix_weights))
    mix_weights = [(part, whole(*part.shape)) for part in mix_weights]
    mix_own = exchange(mix.reshape(8, own, 256), "head")
    residual, feed_copies = kernel_call(
        residual_kernel,
        1,
        ids,
        [(mix_own, whole(8, own, 256))]
        + mix_weights
        + [(layer_input, whole(own, D)), (gains, whole(8, D))],
        [
            (shape(own, D), whole(own, D)),
            (shape(8, own, D, kind=bf16), whole(8, own, D)),
        ],
        flops=2 * own * D * 2048,
    )
    feed_copies, late = lax.optimization_barrier((feed_copies, late))
    feed = rows(exchange(feed_copies, "head"))
    pair_out = shape(2, own, D, kind=bf16), whole(2, own, D)
    *feed_parts, back_part, units, grad_hidden = kernel_call(
        feed_kernel,
        SPAN // FEED_ROWS,
        ids,
        [(feed, blocks(FEED_ROWS, D))]
        + [(part, whole(*part.shape)) for part in span_cot]
        + [(late, whole(D, 768))],
        [pair_out] * 4
        + [
            (shape(SPAN, D, kind=bf16), blocks(FEED_ROWS, D)),
            (shape(SPAN, 256, kind=bf16), blocks(FEED_ROWS, 256)),
            (shape(SPAN, 512, kind=bf16), blocks(FEED_ROWS, 512)),
        ],
        [pltpu.VMEM((FEED_ROWS, D), bf16)],
        flops=2 * SPAN * D * (512 + 256) * 2,
    )
    back_own = exchange(back_part.reshape(8, own, D), "head")
    (feed_grad,) = kernel_call(
        feed_grad_kernel,
        D // GRAD_ROWS,
        ids,
        [
            (feed, lanes(SPAN, GRAD_ROWS)),
            (units, whole(SPAN, 256)),
            (grad_hidden, whole(SPAN, 512)),
        ]
        + [(part, lanes(*part.shape[:-1], GRAD_ROWS)) for part in span_cot],
        [(shape(D, 768, kind=bf16), blocks(GRAD_ROWS, 768))],
        [pltpu.VMEM((SPAN, GRAD_ROWS), bf16)],
        flops=2 * SPAN * D * 768,
    )
    back_own, feed_grad = lax.optimization_barrier((back_own, feed_grad))
    feed_grad = lax.psum_scatter(feed_grad, SEQ, scatter_dimension=0, tiled=True).astype(f32)
    grad_residual, mixed_copies, feed_gain_part, mix_grads = kernel_call(
        mixed_kernel,
        1,
        ids,
        [
            (back_own, whole(8, own, D)),
            (residual, whole(own, D)),
            (cotangent, whole(own, D)),
            (gains, whole(8, D)),
        ]
        + mix_weights,
        [
            (shape(own, D), whole(own, D)),
            (shape(own, D, kind=bf16), whole(own, D)),
            (shape(8, D), whole(8, D)),
            (shape(8, own, 256, kind=bf16), whole(8, own, 256)),
        ],
        flops=2 * own * D * 2048,
    )
    grad_mix = rows(exchange(mix_grads, "head"))
    grad_mix, mixed_copies = lax.optimization_barrier((grad_mix, mixed_copies))
    mixed_beside = beside_y(mixed_copies)
    gy, ggate, do_pad, delta, adjoint, gain_sum = kernel_call(
        gate_back_kernel,
        steps,
        ids,
        [
            (grad_mix, backwards(blocks(ROWS, 256), steps)),
            (y, backwards(blocks(ROWS, WIDE), steps)),
            (gate, backwards(blocks(ROWS, WIDE), steps)),
            (gain_row, whole(1, WIDE)),
            (wr, backwards(blocks(ROWS, 256), steps)),
            (col, backwards(blocks(ROWS, 128), steps)),
            (row, backwards(lanes(24, ROWS), steps)),
            (o_pad, backwards(blocks(ROWS, 128), steps)),
            (pack, pl.BlockSpec((1, 256, 128), lambda i, ids: (0, 4, 0))),
        ],
        [
            (shape(SPAN, WIDE), backwards(blocks(ROWS, WIDE), steps)),
            (shape(SPAN, WIDE, kind=bf16), backwards(blocks(ROWS, WIDE), steps)),
            (shape(SPAN, 128, kind=bf16), backwards(blocks(ROWS, 128), steps)),
            (shape(8, SPAN), backwards(lanes(8, ROWS), steps)),
            (shape(SPANS, 208, 128, kind=bf16), whole(SPANS, 208, 128)),
            (shape(8, WIDE), whole(8, WIDE)),
        ],
        [pltpu.VMEM((WIDE, STATE), f32)],
        flops=2 * SPAN * 256 * 256 * 4,
    )
    adjoint, mixed_beside = lax.optimization_barrier((adjoint, mixed_beside))
    mixed_pair = jnp.stack([mixed_copies, mixed_beside])
    span_mixed = along_x([mixed_pair] * 4)
    adjoints = exchange(adjoint, SEQ)
    back_ins = [
        (do_pad, whole(SPAN, 128)),
        (lse, whole(8, SPAN)),
        (delta, whole(8, SPAN)),
    ]
    dkv_shape = shape(CHIPS, SPAN, 128, kind=bf16), blocks(1, SPAN, 128)
    dkv_other, dq = kernel_call(
        attend_back_other_kernel,
        CHIPS,
        ids,
        [(q, whole(SPAN, 128)), (other, kv_spec)] + back_ins,
        [dkv_shape, (shape(128, SPAN), whole(128, SPAN))],
        flops=2 * 5 * SPAN * SPAN * 256 * 5,
    )
    dq, adjoints, span_mixed, feed_parts = lax.optimization_barrier(
        (dq, adjoints, span_mixed, feed_parts)
    )
    feed_parts = along_x(feed_parts)
    dkv_other = other_core(dkv_other)
    early_part, sums = kernel_call(
        scan_back_kernel,
        steps,
        ids,
        [
            (x, backwards(blocks(ROWS, WIDE), steps)),
            (gy, backwards(blocks(ROWS, WIDE), steps)),
            (wr, backwards(blocks(ROWS, 256), steps)),
            (col, backwards(blocks(ROWS, 128), steps)),
            (row, backwards(lanes(24, ROWS), steps)),
            (entries, backwards(blocks(PER, WIDE, STATE), steps)),
            (adjoints, whole(SPANS, 208, 128)),
            (params, whole(8, 128)),
            (ggate, backwards(blocks(ROWS, WIDE), steps)),
        ],
        [
            (shape(SPAN, 768, kind=bf16), backwards(blocks(ROWS, 768), steps)),
            (shape(8, 128), whole(8, 128)),
        ],
        [pltpu.VMEM((WIDE, STATE), f32)],
        flops=2 * SPAN * 256 * 256 * 16,
    )
    vector = jnp.concatenate(
        [gain_sum[0, :192], sums[:HEADS, 0], sums[:HEADS, 1], jnp.zeros((58,), f32)]
    ).reshape(64, 4)
    high = lax.reduce_precision(vector, 8, 7)
    vector = jnp.concatenate([high, vector - high], axis=1)
    vector = jnp.pad(jnp.tile(vector, (GRAD_ROWS // 64, 1)), ((0, 0), (90, 30)))
    (early_grad,) = kernel_call(
        early_grad_kernel,
        D // GRAD_ROWS,
        ids,
        [
            (normed, lanes(SPAN, GRAD_ROWS)),
            (early_part, whole(SPAN, 768)),
            (mix, whole(SPAN, 256)),
            (feed_gain_part, lanes(8, GRAD_ROWS)),
            (vector, whole(GRAD_ROWS, 128)),
        ]
        + [(part, lanes(*part.shape[:-1], GRAD_ROWS)) for part in span_mixed],
        [(shape(D, 1024, kind=bf16), blocks(GRAD_ROWS, 1024))],
        [pltpu.VMEM((SPAN, GRAD_ROWS), bf16)],
        flops=2 * SPAN * D * 1024,
    )
    dq, early_grad = lax.optimization_barrier((dq, early_grad))
    early_grad = jnp.sum(
        exchange(early_grad.reshape(SPANS, -1, 1024), SEQ).astype(f32), axis=0
    )
    dkv_same, gq = kernel_call(
        attend_back_same_kernel,
        CHIPS,
        ids,
        [(q, whole(SPAN, 128)), (same, kv_spec)] + back_ins
        + [(dq, whole(128, SPAN)), (dkv_other, blocks(1, SPAN, 128))],
        [dkv_shape, (shape(SPAN, 128, kind=bf16), whole(SPAN, 128))],
        [pltpu.VMEM((128, SPAN), f32)],
        flops=2 * 5 * SPAN * SPAN * 256 * 5,
    )
    dkv_same, early_grad, feed_grad, feed_parts = lax.optimization_barrier(
        (dkv_same, early_grad, feed_grad, feed_parts)
    )
    dkv_own = exchange(dkv_same, "chip")
    *normed_parts, mixer_gain_part = kernel_call(
        normed_back_kernel,
        SPAN // CHUNK,
        ids,
        [
            (early_part, blocks(CHUNK, 768)),
            (gq, blocks(CHUNK, 128)),
            (early, whole(D, 768)),
            (normed, blocks(CHUNK, D)),
            (gains, whole(8, D)),
        ],
        [pair_out] * 4 + [(shape(8, D), whole(8, D))],
        [pltpu.VMEM((CHUNK, 768), bf16)],
        flops=2 * SPAN * D * 768,
    )
    feed_own, feed_beside = sum_along_x(feed_parts, ids)
    feed_beside = beside_y(feed_beside)
    layer_output = (residual + feed_own + feed_beside.astype(f32)).astype(bf16)
    dkv_own = jnp.sum(dkv_own.astype(f32), axis=0).astype(bf16)
    normed_parts = along_x(normed_parts)
    gkv = exchange(dkv_own.reshape(8, own, 128), "head")
    (attend_grads,) = kernel_call(
        attend_grad_kernel,
        D // GRAD_ROWS,
        ids,
        [
            (normed, lanes(SPAN, GRAD_ROWS)),
            (gq, whole(SPAN, 128)),
            (dkv_own, whole(SPAN, 128)),
            (early, pl.BlockSpec((GRAD_ROWS, 256), lambda i, ids: (i, 3))),
            (gains, lanes(8, GRAD_ROWS)),
            (mixer_gain_part, lanes(8, GRAD_ROWS)),
        ],
        [(shape(D, 384, kind=bf16), blocks(GRAD_ROWS, 384))],
        flops=2 * SPAN * D * 640,
    )
    gkv, attend_grads, normed_parts = lax.optimization_barrier((gkv, attend_grads, normed_parts))
    attend_grads = exchange(attend_grads.reshape(SPANS, -1, 384), SEQ)
    normed_own, normed_beside = sum_along_x(normed_parts, ids)
    normed_beside = beside_y(normed_beside)
    (input_grad,) = kernel_call(
        input_kernel,
        1,
        ids,
        [
            (gkv, whole(8, own, 128)),
            (early, pl.BlockSpec((D, 256), lambda i, ids: (0, 3))),
            (normed_own, whole(own, D)),
            (normed_beside, whole(own, D)),
            (layer_input, whole(own, D)),
            (gains, whole(8, D)),
            (grad_residual, whole(own, D)),
        ],
        [(shape(own, D), whole(own, D))],
        flops=2 * own * D * 256,
    )
    attend_grads = jnp.sum(attend_grads.astype(f32), axis=0)
    common_grad = jnp.concatenate(
        [early_grad[:, 448:472], attend_grads[:, :1], early_grad[:, 473:768], attend_grads[:, 128:]],
        axis=1,
    )
    common_grad = jnp.sum(
        exchange(common_grad.astype(bf16).reshape(8, 8, 576), "head").astype(f32), axis=0
    )
    vector = (early_grad[:, 474:478] + early_grad[:, 478:482]).reshape(256)
    return (
        layer_output,
        input_grad,
        jnp.concatenate([common_grad[:, 64:], common_grad[:, :24]], axis=1),
        common_grad[:, 24],
        common_grad[:, 25],
        jnp.stack([early_grad[:, :192], early_grad[:, 256:448]], axis=1),
        attend_grads[:, 64:128],
        early_grad[:, 768:960],
        early_grad[:, 960:],
        feed_grad[:, :512].reshape(-1, 2, 256),
        feed_grad[:, 512:],
        vector[192:195],
        vector[195:198],
        vector[:192],
    )


def solution(mesh):
    devices = mesh.devices.reshape(CHIPS, 2, mesh.shape["head"])
    every = (*SEQ, "head")
    return jax.shard_map(
        shards,
        mesh=jax.sharding.Mesh(devices, every),
        in_specs=(
            P(every, None),
            P(every, None),
            P(every),
            P(every),
            P(SEQ, None, "head"),
            P(SEQ, "head"),
            P(SEQ, "head"),
            P(SEQ, "head"),
            P(SEQ, None, "head"),
            P(SEQ, "head"),
            P("head"),
            P("head"),
            P("head"),
            P(every, None),
        ),
        out_specs=(
            P(every, None),
            P(every, None),
            P(every, None),
            P(every),
            P(every),
            P(SEQ, None, "head"),
            P(SEQ, "head"),
            P(SEQ, "head"),
            P(SEQ, "head"),
            P(SEQ, None, "head"),
            P(SEQ, "head"),
            P("head"),
            P("head"),
            P("head"),
        ),
        check_vma=False,
    )
```
